256 devices in a mesh: kz: 4 (over y_hi, core), pw: 64 (over x, y_lo, z).
Axes of the slice: x: 4, y: 4 (y_hi: 2, y_lo: 2; y = y_hi * 2 + y_lo), z: 8, core: 2. Of those that a mesh axis runs over, the one named last changes fastest.
Arguments:
- waves: bfloat16 [16, 1, 16384, 2, 256], P('kz', None, 'pw'), may hold values from -1.25 to 1.25
- pw_map: int32 [1, 16384], P(None, 'pw'), may hold values from 0 to 16383, each once within a row
Outputs:
- correlation_plus: float32 [16, 1, 2, 256, 256], P('kz', None, None, 'pw')
- correlation_minus: float32 [16, 1, 2, 256, 256], P('kz', None, None, 'pw')
The draws below stay inside these ranges and needn't reach their ends.
Inputs may be any that keep to these rules, and one draw needn't show every extreme that they name: Each row of pw_map is a permutation of the 16384 plane waves.
All inputs are finite; a program needn't handle non-finite values.
Results may differ from the reference program's by a relative error of at most 0.0003.
Values may be sent and summed in bfloat16 or wider, within the bound.
No kernel may reach another device: no remote copies, remote signals or barrier semaphores. Data moves between devices by JAX's collectives and lax.ppermute only.
A program may use at most 128 MiB of HBM per device.

```python
import jax
import jax.numpy as jnp
from jax import lax

NB = 256
NPW = 16384
KZ = 16
COLS = 1


def raised(values, stream_key, source, target, parts, factor):
    def block_of(position):
        return (jnp.arange(values.shape[position]) // (values.shape[position] // parts)).reshape((-1,) + (1,) * (values.ndim - 1 - position))

    one_side = jax.random.permutation(stream_key, parts)[block_of(target)]
    far = (block_of(target) + parts // 2) % parts
    return jnp.where((block_of(source) == one_side) | (block_of(source) == far), factor * values, values)


def block_scale(own_key, extent, cuts, least, top_value):
    loudness = 1.0
    for position, parts in cuts:
        steps = jax.random.uniform(jax.random.fold_in(jax.random.fold_in(own_key, 6), position), (parts,), jnp.float32, least / len(cuts), top_value / len(cuts))
        loudness = loudness * jnp.repeat(jnp.exp(steps), extent[position] // parts).reshape((-1,) + (1,) * (len(extent) - 1 - position))
    return loudness


def noise_with(key, extent, deviation, reach, cuts, heavy, held_as=jnp.bfloat16):
    entries = deviation * jax.random.normal(key, extent, jnp.float32)
    if cuts:
        entries = entries * block_scale(key, extent, cuts, -0.22, 0.18)
    return jnp.clip(raised(entries, jax.random.fold_in(key, 3), *heavy), -reach, reach).astype(held_as)


def setup_inputs(seed: int = 0) -> dict:
    key_of = jax.random.split(jax.random.key(seed), 3)
    waves = noise_with(key_of[0], (KZ, COLS, NPW, 2, NB), ((2 * NPW) ** -0.25), 1.25, ((0, 4), (2, 64)), (2, 4, 64, 4.0))
    pw_map = jax.vmap(lambda own: jax.random.permutation(own, NPW))(jax.random.split(key_of[1], COLS)).reshape((COLS, NPW)).astype(jnp.int32)
    return dict(waves=waves, pw_map=pw_map)


def correlation_one(pair):
    left, right = pair
    left = left.astype(jnp.float32)
    right = right.astype(jnp.float32)
    prods = jnp.einsum('cgpn,cgqm->cpqnm', left, right, precision=lax.Precision.HIGHEST)
    real_part = prods[:, 0, 0] + prods[:, 1, 1]
    imag_part = prods[:, 0, 1] - prods[:, 1, 0]
    return jnp.stack([real_part, imag_part], axis=1)


def reference(waves, pw_map):
    first = jnp.take_along_axis(waves[0], pw_map[:, :, None, None], axis=1)
    upper = jnp.concatenate([waves[1:], first[None]], axis=0)
    column_ids = jnp.arange(COLS, dtype=jnp.int32)[:, None]
    inverse = jnp.zeros((COLS, NPW), jnp.int32).at[column_ids, pw_map].set(
        jnp.broadcast_to(jnp.arange(NPW, dtype=jnp.int32)[None, :], (COLS, NPW)))
    last = jnp.take_along_axis(waves[KZ - 1], inverse[:, :, None, None], axis=1)
    lower = jnp.concatenate([last[None], waves[:-1]], axis=0)
    correlation_plus = lax.map(correlation_one, (waves, upper))
    correlation_minus = lax.map(correlation_one, (waves, lower))
    return correlation_plus, correlation_minus
```

```python
import jax
import jax.numpy as jnp
import numpy as np
from jax import lax
from jax.experimental import pallas as pl
from jax.experimental.pallas import tpu as pltpu
from jax.sharding import PartitionSpec as P


def pick_kernel(table_ref, hi_ref, lo_ref, out_ref):
    blocks, width = hi_ref.shape
    parts = table_ref.shape[0] // 2
    table = table_ref[...]
    rows = lax.broadcasted_iota(jnp.int32, (table.shape[1], width), 0)
    owners = lax.broadcasted_iota(jnp.int32, (parts, width), 0)

    def step(t, carry):
        base = pl.multiple_of(t * 8, 8)
        his = hi_ref[pl.ds(base, 8), :]
        los = lo_ref[pl.ds(base, 8), :]
        real_rows, imag_rows = [], []
        for r in range(8):
            hot = jnp.where(rows == los[r : r + 1, :], 1.0, 0.0).astype(jnp.bfloat16)
            found = jnp.dot(table, hot, preferred_element_type=jnp.float32)
            mine = owners == his[r : r + 1, :]
            real_rows.append(jnp.sum(jnp.where(mine, found[:parts], 0.0), axis=0, keepdims=True))
            imag_rows.append(jnp.sum(jnp.where(mine, found[parts:], 0.0), axis=0, keepdims=True))
        out_ref[0, pl.ds(base, 8), :] = jnp.concatenate(real_rows, axis=0)
        out_ref[1, pl.ds(base, 8), :] = jnp.concatenate(imag_rows, axis=0)
        return carry

    lax.fori_loop(0, blocks // 8, step, 0)


def pick(table, hi, lo):
    blocks, width = hi.shape
    vmem = pl.BlockSpec(memory_space=pltpu.VMEM)
    return pl.pallas_call(
        pick_kernel,
        out_shape=jax.ShapeDtypeStruct((2, blocks, width), jnp.float32),
        in_specs=[vmem] * 3,
        out_specs=vmem,
        cost_estimate=pl.CostEstimate(
            flops=2 * table.size * blocks * width, bytes_accessed=table.size * 6, transcendentals=0
        ),
        name="pick",
    )(table, hi, lo)


def turned(planes, axis):
    real, imag = jnp.split(planes, 2, axis=axis)
    return jnp.concatenate([imag, -real], axis=axis)


def body(waves, pw_map):
    kz_dev, cols, rows, _, bands = waves.shape
    n_kz, n_pw = lax.axis_size("kz"), lax.axis_size("pw")
    share = bands // n_pw
    kz_pos = lax.axis_index("kz")
    last = n_kz - 1
    planes = waves[:, 0]
    f32, bf16 = jnp.float32, jnp.bfloat16

    def swap(x):
        return lax.all_to_all(x, "pw", 0, 0, tiled=True)

    def sent(x, pairs):
        return lax.ppermute(x, "kz", pairs)

    with jax.named_scope("deal"):
        order = np.arange(bands).reshape(n_pw, share).T.reshape(-1)
        deal = jnp.asarray(np.eye(bands)[order], dtype=bf16)
        dealt = jnp.einsum("qb,gpb->qpg", deal, planes[0], preferred_element_type=f32)
        dealt = dealt.astype(bf16).reshape(share, n_pw, 2, rows)
        mine = jnp.where(kz_pos == 0, dealt[0], jnp.zeros_like(dealt[0]))
        for j in range(1, n_kz):
            mine = mine + sent(dealt[j], [(0, j)])
        digits = jnp.stack([pw_map[0] // rows, pw_map[0] % rows]).astype(bf16)
        load = jnp.concatenate(
            [mine, jnp.broadcast_to(digits[None], (n_pw, 2, rows))], axis=1
        )
        spread = swap(load)
    with jax.named_scope("pick"):
        table = spread[:, :2].transpose(1, 0, 2).reshape(2 * n_pw, rows)
        hi = spread[:, 2].astype(jnp.int32)
        lo = spread[:, 3].astype(jnp.int32)
        picked = pick(table, hi, lo).astype(bf16)
        moved = swap(picked.transpose(1, 0, 2))

    with jax.named_scope("inner"):
        arriving = sent(planes[0], [((i + 1) % n_kz, i) for i in range(n_kz)])
        right = jnp.concatenate([planes[1:], arriving[None]], axis=0)
        both = jnp.stack([right, turned(right, 2)], axis=1)
        terms = jnp.einsum("kgpn,kogpm->nkom", planes, both, preferred_element_type=f32)
        terms = terms.reshape(n_pw, share * kz_dev * 2, bands)
        total = jnp.sum(swap(terms), axis=0).reshape(share, kz_dev, 2, bands)
        plus = total.transpose(1, 2, 0, 3)

    with jax.named_scope("mirror"):
        signs = jnp.array([1.0, -1.0], f32)[None, :, None, None]
        tiles = (plus * signs).reshape(kz_dev, 2, share, n_pw, share)
        tiles = tiles.transpose(3, 0, 1, 4, 2).reshape(n_pw, -1)
        tiles = swap(tiles).reshape(n_pw, kz_dev, 2, share, share)
        minus = tiles.transpose(1, 2, 3, 0, 4).reshape(kz_dev, 2, share, bands)

    with jax.named_scope("edge"):
        final = planes[kz_dev - 1]
        for j in range(last):
            got = sent(planes[kz_dev - 1], [(last, j)])
            final = jnp.where(kz_pos == j, got, final)
        moved_both = jnp.stack([moved, turned(moved, 1)], axis=1)
        rows_n = jnp.einsum("gpn,iopg->noi", final, moved_both, preferred_element_type=f32)
        final_both = jnp.stack([final, turned(final, 1)], axis=0)
        rows_m = jnp.einsum("ipg,ogpn->ion", moved, final_both, preferred_element_type=f32)
        out = jnp.concatenate([rows_n.reshape(n_pw, -1), rows_m.reshape(n_pw, -1)], axis=1)
        edge = jnp.sum(swap(out), axis=0)
        half = edge.shape[0] // 2
        edge_n, edge_m = edge[:half], edge[half:]

    with jax.named_scope("close"):
        edge_ns, edge_ms = [], []
        for j in range(n_kz):
            edge_ns.append(edge_n if j == last else sent(edge_n, [(j, last)]))
            edge_ms.append(edge_m if j == 0 else sent(edge_m, [(j, 0)]))
        last_plus = jnp.stack(edge_ns).reshape(share, share, 2, n_pw)
        last_plus = last_plus.transpose(2, 1, 3, 0).reshape(2, share, bands)
        first_minus = jnp.stack(edge_ms).reshape(share, 2, bands).transpose(1, 0, 2)
        before = sent(minus[kz_dev - 1], [(i, i + 1) for i in range(last)])
        first = jnp.where(kz_pos == 0, first_minus, before)
        plus_end = jnp.where(kz_pos == last, last_plus, plus[kz_dev - 1])
        plus = jnp.concatenate([plus[:-1], plus_end[None]], axis=0)
        minus = jnp.concatenate([first[None], minus[:-1]], axis=0)
    return plus[:, None], minus[:, None]


def solution(mesh):
    return jax.shard_map(
        body,
        mesh=mesh,
        in_specs=(P("kz", None, "pw", None, None), P(None, "pw")),
        out_specs=(P("kz", None, None, "pw", None), P("kz", None, None, "pw", None)),
        check_vma=False,
    )
```

```python
import jax
import jax.numpy as jnp
from jax import lax
from jax.experimental import pallas as pl
from jax.experimental.pallas import tpu as pltpu
from jax.sharding import Mesh, PartitionSpec as P

KZ = ("y_hi", "core")
PW = ("x", "y_lo", "z")
F32, BF16 = jnp.float32, jnp.bfloat16
VMEM = pl.BlockSpec(memory_space=pltpu.VMEM)
AFTER = pl.BlockSpec(memory_space=pl.ANY)
LANES = 128


def iota(shape, axis):
    return lax.broadcasted_iota(jnp.int32, shape, axis)


def across(left, right, dims, precision=None):
    return lax.dot_general(left, right, (dims, ((), ())), precision=precision, preferred_element_type=F32)


def placed(left, right, dims):
    return across(left, right, dims, lax.Precision.HIGHEST)


def wide(real, imag):
    return jnp.concatenate(
        [jnp.concatenate([real, imag], axis=1), jnp.concatenate([imag, -real], axis=1)], axis=0
    )


def call(kernel, name, outs, operands, after=(), flops=0, scratch=(), far=()):
    outs = [jax.ShapeDtypeStruct(*o) if i in far else pltpu.VMEM(*o) for i, o in enumerate(outs)]
    size = sum(x.size * x.dtype.itemsize for x in operands)
    return pl.pallas_call(
        kernel,
        out_shape=outs,
        in_specs=[AFTER] * len(after) + [VMEM] * len(operands),
        out_specs=[VMEM] * len(outs),
        scratch_shapes=list(scratch),
        cost_estimate=pl.CostEstimate(flops=flops, bytes_accessed=2 * size, transcendentals=0),
        compiler_params=pltpu.CompilerParams(vmem_limit_bytes=16 << 20),
        name=name,
    )(*after, *(pltpu.with_memory_space_constraint(x, pltpu.VMEM) for x in operands))


def deal_kernel(planes_ref, *out_refs):
    groups = len(out_refs) - 1
    plane_ref = planes_ref.at[0]
    bands = plane_ref.shape[2]
    blocks = bands // groups
    place, band = iota((bands, bands), 0), iota((bands, bands), 1)
    order = jnp.where(band == (place % blocks) * groups + place // blocks, 1.0, 0.0).astype(BF16)
    for part in range(2):
        dealt = across(order, plane_ref[part], ((1,), (1,))).astype(BF16)
        for j in range(groups):
            out_refs[j][pl.ds(part * blocks, blocks), :] = dealt[j * blocks : (j + 1) * blocks]
    out_refs[groups][...] = plane_ref[...]


def terms_kernel(planes_ref, arriving_ref, *refs):
    out_refs, last_ref, prod_ref = refs[:-2], refs[-2], refs[-1]
    count, _, rows, bands = planes_ref.shape
    blocks, share = out_refs[0].shape[0], out_refs[0].shape[1] * LANES // (count * 2 * bands)
    per = 2 * bands // LANES
    here = lax.axis_index("x")
    for k in range(count):
        left = planes_ref[k].reshape(2 * rows, bands)
        after = arriving_ref if k == count - 1 else planes_ref.at[k + 1]
        prod_ref[...] = across(left, wide(after[0], after[1]), ((0,), (0,)))
        for d, out_ref in enumerate(out_refs):
            to = lax.rem(here + d, len(out_refs))
            base = pl.multiple_of(to * blocks * share, blocks * share)
            mine = prod_ref.at[pl.ds(base, blocks * share)]
            for b in range(blocks):
                for c in range(per):
                    piece = mine[pl.ds(b * share, share), pl.ds(c * LANES, LANES)]
                    out_ref[b, pl.ds((k * per + c) * share, share), :] = piece
    last_ref[...] = planes_ref[count - 1]


def load_kernel(after_ref, map_ref, own_ref, *refs):
    out_ref = refs[-1]
    blocks = out_ref.shape[0]
    first = jnp.where(lax.axis_index(KZ) == 0, 1.0, 0.0)
    mine = own_ref[...].astype(F32) * first
    for ref in refs[:-1]:
        mine = mine + ref[...].astype(F32)
    width = mine.shape[1]
    index = map_ref[...]
    digits = [(index // width).astype(F32), (index % width).astype(F32)]
    parts = [mine[:blocks], mine[blocks:]] + [jnp.broadcast_to(d, (blocks, width)) for d in digits]
    per = width // LANES
    for i, part in enumerate(parts):
        for c in range(per):
            out_ref[:, i * per + c, :] = part[:, c * LANES : (c + 1) * LANES]


def pick_kernel(spread_ref, out_ref, hi_ref, lo_ref):
    blocks, width = hi_ref.shape
    per = width // LANES

    def part(i):
        return jnp.concatenate([spread_ref[:, i * per + c, :] for c in range(per)], axis=1)

    table = jnp.concatenate([part(0), part(1)], axis=0).astype(BF16)
    hi_ref[...] = part(2).astype(jnp.int32)
    lo_ref[...] = part(3).astype(jnp.int32)
    rows, owners = iota((width, width), 0), iota((blocks, width), 0)

    def step(t, carry):
        base = pl.multiple_of(t * 8, 8)
        his, los = hi_ref[pl.ds(base, 8), :], lo_ref[pl.ds(base, 8), :]
        real_rows, imag_rows = [], []
        for r in range(8):
            hot = jnp.where(rows == los[r : r + 1, :], 1.0, 0.0).astype(BF16)
            found = jnp.dot(table, hot, preferred_element_type=F32)
            mine = owners == his[r : r + 1, :]
            real_rows.append(jnp.sum(jnp.where(mine, found[:blocks], 0.0), axis=0, keepdims=True))
            imag_rows.append(jnp.sum(jnp.where(mine, found[blocks:], 0.0), axis=0, keepdims=True))
        for i, picked in enumerate((real_rows, imag_rows)):
            picked = jnp.concatenate(picked, axis=0)
            for c in range(per):
                out_ref[pl.ds(base, 8), i * per + c, :] = picked[:, c * LANES : (c + 1) * LANES]
        return carry

    lax.fori_loop(0, blocks // 8, step, 0)


def halve_kernel(after_ref, *refs):
    sums_refs, (keep_ref, give_ref) = refs[:-2], refs[-2:]
    half = keep_ref.shape[0]
    here = lax.axis_index("y_lo")
    for out_ref, side in ((keep_ref, here), (give_ref, 1 - here)):
        total = sums_refs[0][pl.ds(side * half, half)]
        for ref in sums_refs[1:]:
            total = total + ref[pl.ds(side * half, half)]
        out_ref[...] = total


def merge_kernel(*refs):
    picked_ref, keep_ref, got_ref, out_ref = refs[-4:]
    far = keep_ref.shape[0]
    near, chunks = picked_ref.shape[0] // far, picked_ref.shape[1]
    for p in range(near):
        for z in range(far):
            out_ref[z, pl.ds(p * chunks, chunks), :] = picked_ref[p * far + z]
    out_ref[:, pl.ds(near * chunks, keep_ref.shape[1]), :] = keep_ref[...] + got_ref[...]


def edge_kernel(got_ref, own_ref, *refs):
    sent_refs, (plus_ref, out_ref, moved_ref, turn_ref, rows_ref) = refs[:-5], refs[-5:]
    count, _, share, bands = plus_ref.shape
    blocks, width = moved_ref.shape
    far = got_ref.shape[0]
    chunks, near, per = width // LANES, blocks // far, bands // LANES
    here = lax.axis_index(KZ)

    total = got_ref[0, pl.ds(near * chunks, count * 2 * per * share), :]
    for z in range(1, far):
        total = total + got_ref[z, pl.ds(near * chunks, count * 2 * per * share), :]
    for k in range(count):
        for o in range(2):
            for c in range(per):
                first = ((k * 2 + o) * per + c) * share
                piece = total[first : first + share]
                plus_ref[k, o, :, pl.ds(c * LANES, LANES)] = piece
                rows_ref[pl.ds((k * 2 + o) * share, share), pl.ds(c * LANES, LANES)] = piece
    place, band = iota((bands, bands), 0), iota((bands, bands), 1)
    order = jnp.where(band == (place % blocks) * share + place // blocks, 1.0, 0.0)
    tiles = placed(order, rows_ref[...], ((1,), (1,)))
    tiles = jnp.concatenate([tiles[i * blocks : (i + 1) * blocks] for i in range(share)], axis=1)
    out_ref[pl.ds(8, blocks, stride=9), :] = tiles

    final = own_ref[...]
    for j, ref in enumerate(sent_refs):
        final = jnp.where(here == j, ref[...], final)
    for p in range(near):
        for c in range(chunks):
            moved_ref[pl.ds(p * far, far), pl.ds(c * LANES, LANES)] = got_ref[:, p * chunks + c, :]
    moved = moved_ref[...].astype(BF16)
    prods = jnp.dot(moved, wide(final[0], final[1]), preferred_element_type=F32)
    turn_ref[...] = jnp.concatenate([prods[:, :bands].T, -prods[:, bands:].T], axis=1)
    for c in range(4):
        out_ref[pl.ds(c, blocks, stride=9), :] = turn_ref[pl.ds(c, blocks, stride=4), :]
        out_ref[pl.ds(4 + c, blocks, stride=9), :] = prods[:, LANES * c : LANES * (c + 1)]


def gather_kernel(back_ref, minus_ref, *pay_refs):
    count, _, share, bands = minus_ref.shape
    blocks = back_ref.shape[0] // 9
    groups = len(pay_refs)
    sums = [jnp.sum(back_ref[pl.ds(c, blocks, stride=9), :], axis=0, keepdims=True) for c in range(8)]
    edge_n, edge_m = jnp.concatenate(sums[:4], axis=0), jnp.concatenate(sums[4:], axis=0)
    tiles = back_ref[pl.ds(8, blocks, stride=9), :]
    lane = iota((blocks, bands), 1)
    spread = placed(tiles, jnp.where(lane // share == iota((blocks, bands), 0), 1.0, 0.0), ((0,), (0,)))
    spread = jnp.where(iota(spread.shape, 0) % share == iota(spread.shape, 1) % share, spread, 0.0)
    shape = (count * 2 * share, spread.shape[0])
    row, col = iota(shape, 0), iota(shape, 1)
    same = (row % share == col // (count * 2 * share)) & (row // share == (col // share) % (count * 2))
    sign = jnp.where((row // share) % 2 == 0, 1.0, -1.0)
    mirror = placed(jnp.where(same, sign, 0.0), spread, ((1,), (0,)))
    for k in range(count):
        for o in range(2):
            minus_ref[k, o] = mirror[(2 * k + o) * share : (2 * k + o + 1) * share]
    for d, ref in enumerate(pay_refs):
        piece = jnp.where(lax.rem(lax.axis_index(KZ) + d, groups) == groups - 1, edge_n, edge_m)
        if d == 1:
            ref[...] = jnp.zeros_like(ref)
            ref[pl.ds(0, 2 * share), :] = mirror[(count - 1) * 2 * share :]
            ref[pl.ds(2 * share, share), pl.ds(0, LANES)] = piece
        else:
            ref[...] = piece


def close_kernel(plus_ref, minus_ref, *refs):
    got_refs, plus_out, minus_out = refs[:-2], refs[-2], refs[-1]
    count, _, share, bands = plus_ref.shape
    groups = len(got_refs)
    here = lax.axis_index(KZ)
    got = [
        ref[pl.ds(2 * share, share), pl.ds(0, LANES)] if d == 1 else ref[...]
        for d, ref in enumerate(got_refs)
    ]
    plus_out[...] = plus_ref[...]
    for k in range(1, count):
        minus_out[k] = minus_ref[k - 1]
    for o in range(2):
        minus_out[0, o] = got_refs[1][pl.ds(o * share, share), :]

    @pl.when(here == groups - 1)
    def _():
        shape = (LANES, 2 * bands)
        row, col = iota(shape, 0), iota(shape, 1)
        half = LANES // 2
        rows = jnp.zeros((share, 2 * bands), F32)
        for j in range(groups):
            spot = (row // half == col // bands) & ((row % half) * groups + j == col % bands)
            rows = rows + placed(got[groups - 1 - j], jnp.where(spot, 1.0, 0.0), ((1,), (0,)))
        for o in range(2):
            plus_out[count - 1, o] = rows[:, o * bands : (o + 1) * bands]

    @pl.when(here == 0)
    def _():
        per = bands // LANES
        for j in range(groups):
            piece = got[(groups - j) % groups]
            for r in range(2 * per):
                minus_out[0, r // per, pl.ds(j, 1), pl.ds((r % per) * LANES, LANES)] = piece[r : r + 1]


def body(waves, pw_map):
    kz_dev, _, rows, _, bands = waves.shape
    n_kz, n_pw, n_x, n_z = (lax.axis_size(a) for a in (KZ, PW, "x", "z"))
    share, group = bands // n_pw, n_pw // n_x
    planes = waves[:, 0].transpose(0, 2, 1, 3)

    def swap(x, axes):
        return lax.all_to_all(x, axes, 0, 0, tiled=True)

    def sent(x, pairs):
        return lax.ppermute(x, KZ, pairs)

    def around(x, d):
        return sent(x, [(i, (i + d) % n_kz) for i in range(n_kz)])

    def along(x, d):
        return lax.ppermute(x, "x", [(i, (i + d) % n_x) for i in range(n_x)])

    plane = (planes.shape[1:], BF16)
    with jax.named_scope("deal"):
        *dealt, first = call(
            deal_kernel, "deal", [((2 * n_pw, rows), BF16)] * share + [plane], (planes,),
            flops=4 * rows * bands * bands,
        )
        dealt = [dealt[0]] + [sent(dealt[j], [(0, j)]) for j in range(1, n_kz)]

    with jax.named_scope("inner"):
        arriving = around(first, n_kz - 1)
        chunks = kz_dev * 2 * bands * share // LANES
        *terms, final = call(
            terms_kernel, "terms", [((group, chunks, LANES), F32)] * n_x + [plane], (planes, arriving),
            flops=kz_dev * 8 * rows * bands * bands, scratch=[pltpu.VMEM((bands, 2 * bands), F32)],
        )
        sums = [terms[0]] + [along(terms[d], d) for d in range(1, n_x)]
        finals = [sent(final, [(n_kz - 1, j)]) for j in range(n_kz - 1)]

    with jax.named_scope("deal"):
        (load,) = call(
            load_kernel, "load", [((n_pw, 4 * rows // LANES, LANES), F32)], (pw_map, *dealt),
            after=(terms[0],), far=(0,),
        )
        spread = swap(load, PW)
    with jax.named_scope("pick"):
        (picked,) = call(
            pick_kernel, "pick", [((n_pw, 2 * rows // LANES, LANES), F32)], (spread,),
            flops=4 * n_pw * n_pw * rows * rows, scratch=[pltpu.VMEM((n_pw, rows), jnp.int32)] * 2, far=(0,),
        )

    with jax.named_scope("inner"):
        keep, give = call(
            halve_kernel, "halve", [((n_z, chunks, LANES), F32)] * 2, sums, after=(picked,)
        )
        halves = (keep, lax.ppermute(give, "y_lo", [(0, 1), (1, 0)]))
    with jax.named_scope("pick"):
        picked = swap(picked, ("x", "y_lo"))
    with jax.named_scope("inner"):
        (merged,) = call(
            merge_kernel, "merge", [((n_z, n_pw // n_z * 2 * rows // LANES + chunks, LANES), F32)],
            (picked, *halves), after=finals, far=(0,),
        )
        got = swap(merged, "z")

    with jax.named_scope("edge"):
        rows_out = ((kz_dev, 2, share, bands), F32)
        plus, out = call(
            edge_kernel, "edge", [rows_out, ((n_pw * 9, LANES), F32)], (got, final, *finals),
            flops=8 * n_pw * rows * bands, far=(1,),
            scratch=[
                pltpu.VMEM((n_pw, 2 * rows), F32),
                pltpu.VMEM((bands, 2 * n_pw), F32),
                pltpu.VMEM((kz_dev * 2 * share, bands), F32),
            ],
        )
        back = swap(out.reshape(n_pw, 1, 9 * LANES), PW).reshape(n_pw * 9, LANES)

    with jax.named_scope("close"):
        piece = ((share, LANES), F32)
        long = ((4 * share, bands), F32)
        minus, *pieces = call(gather_kernel, "gather", [rows_out, piece, long] + [piece] * (n_kz - 2), (back,))
        pieces = [pieces[0]] + [around(pieces[d], d) for d in range(1, n_kz)]
        plus, minus = call(close_kernel, "close", [rows_out] * 2, (plus, minus, *pieces), far=(0, 1))
    return plus[:, None], minus[:, None]


def solution(mesh):
    fine = Mesh(mesh.devices.reshape(2, 2, 4, 2, 8), KZ + PW)
    out = P(KZ, None, None, PW, None)
    return jax.shard_map(
        body,
        mesh=fine,
        in_specs=(P(KZ, None, PW, None, None), P(None, PW)),
        out_specs=(out, out),
        check_vma=False,
    )
```

```python
import jax
import jax.numpy as jnp
from jax import lax
from jax.experimental import pallas as pl
from jax.experimental.pallas import tpu as pltpu
from jax.sharding import Mesh, PartitionSpec as P

KZ = ("y_hi", "core")
PW = ("x", "y_lo", "z")
F32, BF16 = jnp.float32, jnp.bfloat16
VMEM = pl.BlockSpec(memory_space=pltpu.VMEM)
AFTER = pl.BlockSpec(memory_space=pl.ANY)
LANES = 128


def iota(shape, axis):
    return lax.broadcasted_iota(jnp.int32, shape, axis)


def across(left, right, dims, precision=None):
    return lax.dot_general(left, right, (dims, ((), ())), precision=precision, preferred_element_type=F32)


def placed(left, right, dims):
    return across(left, right, dims, lax.Precision.HIGHEST)


def wide(real, imag):
    return jnp.concatenate(
        [jnp.concatenate([real, imag], axis=1), jnp.concatenate([imag, -real], axis=1)], axis=0
    )


def call(kernel, name, outs, operands, after=(), flops=0, scratch=(), far=()):
    outs = [jax.ShapeDtypeStruct(*o) if i in far else pltpu.VMEM(*o) for i, o in enumerate(outs)]
    size = sum(x.size * x.dtype.itemsize for x in operands)
    return pl.pallas_call(
        kernel,
        out_shape=outs,
        in_specs=[AFTER] * len(after) + [VMEM] * len(operands),
        out_specs=[VMEM] * len(outs),
        scratch_shapes=list(scratch),
        cost_estimate=pl.CostEstimate(flops=flops, bytes_accessed=2 * size, transcendentals=0),
        compiler_params=pltpu.CompilerParams(vmem_limit_bytes=16 << 20),
        name=name,
    )(*after, *(pltpu.with_memory_space_constraint(x, pltpu.VMEM) for x in operands))


def dealt_to(group, groups, bands):
    shape = (bands // groups, bands)
    return jnp.where(iota(shape, 1) == iota(shape, 0) * groups + group, 1.0, 0.0).astype(BF16)


def deal_kernel(planes_ref, map_ref, *out_refs):
    digits_ref, first_ref, out_refs = out_refs[-1], out_refs[-2], out_refs[:-2]
    groups, width, bands = len(out_refs) + 1, planes_ref.shape[2], planes_ref.shape[3]
    blocks = bands // groups
    for j, out_ref in enumerate(out_refs):
        for part in range(2):
            dealt = across(dealt_to(j, groups, bands), planes_ref[0, part], ((1,), (1,)))
            out_ref[pl.ds(part * blocks, blocks), :] = dealt.astype(BF16)
    first_ref[...] = planes_ref[0]
    index = map_ref[...]
    per = width // LANES
    for i, digit in enumerate((index // width, index % width)):
        for c in range(per):
            digits_ref[pl.ds(i * per + c, 1), :] = digit[:, c * LANES : (c + 1) * LANES].astype(F32)


def terms_kernel(*refs):
    planes_ref, arriving_ref, *along_refs = refs[-8:-4]
    beside_refs, last_ref, prod_ref = refs[-4:-2], refs[-2], refs[-1]
    count, _, rows, bands = planes_ref.shape
    half, per = count // 2, 2 * bands // LANES
    size = along_refs[0].shape[0] // 4
    share = bands // (8 * size)
    here, side = lax.axis_index("x"), lax.axis_index("y_lo")
    near = here + 1 - 2 * lax.rem(here, 2)
    sides = (side, 1 - side)
    for k in range(count):
        left = planes_ref[k].reshape(2 * rows, bands)
        after = arriving_ref if k == count - 1 else planes_ref.at[k + 1]
        prod_ref[...] = across(left, wide(after[0], after[1]), ((0,), (0,)))
        if k < half:
            order = [[(x, s) for x in xs for s in sides] for xs in ((here, 3 - here), (near, 3 - near))]
        else:
            order = [[(x, s) for x in (here, 3 - here, near, 3 - near)] for s in sides]
        for out_ref, places in zip(along_refs if k < half else beside_refs, order):
            for p, (x, s) in enumerate(places):
                first = pl.multiple_of((2 * x + s) * size * share, size * share)
                mine = prod_ref.at[pl.ds(first, size * share)]
                for i in range(size):
                    for c in range(per):
                        piece = mine[pl.ds(i * share, share), pl.ds(c * LANES, LANES)]
                        out_ref[p * size + i, pl.ds(((k % half) * per + c) * share, share), :] = piece
    last_ref[...] = planes_ref[count - 1]


def load_kernel(after_ref, digits_ref, own_ref, arriving_ref, *refs):
    out_ref = refs[-1]
    blocks = out_ref.shape[0]
    here, groups = lax.axis_index(KZ), len(refs) + 1
    mine = jnp.where(here == 0, own_ref[...].astype(F32), 0.0)
    for ref in refs[:-1]:
        mine = mine + ref[...].astype(F32)
    order = dealt_to(groups - 1, groups, arriving_ref.shape[2])
    last = [across(order, arriving_ref[part], ((1,), (1,))) for part in range(2)]
    mine = jnp.where(here == groups - 1, jnp.concatenate(last, axis=0), mine)
    per = mine.shape[1] // LANES
    for i, part in enumerate((mine[:blocks], mine[blocks:])):
        for c in range(per):
            out_ref[:, i * per + c, :] = part[:, c * LANES : (c + 1) * LANES]
    digits = digits_ref[...]
    for c in range(2 * per):
        out_ref[:, 2 * per + c, :] = jnp.broadcast_to(digits[c : c + 1], (blocks, LANES))


def pick_kernel(spread_ref, out_ref, hi_ref, lo_ref):
    blocks, width = hi_ref.shape
    per = width // LANES

    def part(i):
        return jnp.concatenate([spread_ref[:, i * per + c, :] for c in range(per)], axis=1)

    table = jnp.concatenate([part(0), part(1)], axis=0).astype(BF16)
    hi_ref[...] = part(2).astype(jnp.int32)
    lo_ref[...] = part(3).astype(jnp.int32)
    rows, owners = iota((width, width), 0), iota((blocks, width), 0)

    def step(t, carry):
        base = pl.multiple_of(t * 8, 8)
        his, los = hi_ref[pl.ds(base, 8), :], lo_ref[pl.ds(base, 8), :]
        real_rows, imag_rows = [], []
        for r in range(8):
            hot = jnp.where(rows == los[r : r + 1, :], 1.0, 0.0).astype(BF16)
            found = jnp.dot(table, hot, preferred_element_type=F32)
            mine = owners == his[r : r + 1, :]
            real_rows.append(jnp.sum(jnp.where(mine, found[:blocks], 0.0), axis=0, keepdims=True))
            imag_rows.append(jnp.sum(jnp.where(mine, found[blocks:], 0.0), axis=0, keepdims=True))
        for i, picked in enumerate((real_rows, imag_rows)):
            picked = jnp.concatenate(picked, axis=0)
            for c in range(per):
                out_ref[pl.ds(base, 8), i * per + c, :] = picked[:, c * LANES : (c + 1) * LANES]
        return carry

    lax.fori_loop(0, blocks // 8, step, 0)


def fold_kernel(*refs):
    in_refs, out_refs = refs[:4], refs[4:]
    half = out_refs[0].shape[0]
    for i in range(4):
        kept, got = in_refs[i // 2 * 2], in_refs[i // 2 * 2 + 1]
        part = pl.ds(i % 2 * half, half)
        out_refs[i][...] = kept[part] + got[part]


def merge_kernel(*refs):
    picked_ref, sums_refs, out_ref = refs[-6], refs[-5:-1], refs[-1]
    far, rows = out_ref.shape[0], sums_refs[0].shape[1]
    near, chunks = picked_ref.shape[0] // far, picked_ref.shape[1]
    for p in range(near):
        for z in range(far):
            out_ref[z, pl.ds(p * chunks, chunks), :] = picked_ref[p * far + z]
    for i in range(2):
        out_ref[:, pl.ds(near * chunks + i * rows, rows), :] = sums_refs[2 * i][...] + sums_refs[2 * i + 1][...]


def edge_kernel(got_ref, own_ref, *refs):
    sent_refs, (plus_ref, out_ref, moved_ref, turn_ref, rows_ref) = refs[:-5], refs[-5:]
    count, _, share, bands = plus_ref.shape
    blocks, width = moved_ref.shape
    far = got_ref.shape[0]
    chunks, near, per = width // LANES, blocks // far, bands // LANES
    here = lax.axis_index(KZ)

    total = got_ref[0, pl.ds(near * chunks, count * 2 * per * share), :]
    for z in range(1, far):
        total = total + got_ref[z, pl.ds(near * chunks, count * 2 * per * share), :]
    for k in range(count):
        for o in range(2):
            for c in range(per):
                first = ((k * 2 + o) * per + c) * share
                piece = total[first : first + share]
                plus_ref[k, o, :, pl.ds(c * LANES, LANES)] = piece
                rows_ref[pl.ds((k * 2 + o) * share, share), pl.ds(c * LANES, LANES)] = piece
    place, band = iota((bands, bands), 0), iota((bands, bands), 1)
    order = jnp.where(band == (place % blocks) * share + place // blocks, 1.0, 0.0)
    tiles = placed(order, rows_ref[...], ((1,), (1,)))
    tiles = jnp.concatenate([tiles[i * blocks : (i + 1) * blocks] for i in range(share)], axis=1)
    out_ref[pl.ds(8, blocks, stride=9), :] = tiles

    final = own_ref[...]
    for j, ref in enumerate(sent_refs):
        final = jnp.where(here == j, ref[...], final)
    for p in range(near):
        for c in range(chunks):
            moved_ref[pl.ds(p * far, far), pl.ds(c * LANES, LANES)] = got_ref[:, p * chunks + c, :]
    moved = moved_ref[...].astype(BF16)
    prods = jnp.dot(moved, wide(final[0], final[1]), preferred_element_type=F32)
    turn_ref[...] = jnp.concatenate([prods[:, :bands].T, -prods[:, bands:].T], axis=1)
    for c in range(4):
        out_ref[pl.ds(c, blocks, stride=9), :] = turn_ref[pl.ds(c, blocks, stride=4), :]
        out_ref[pl.ds(4 + c, blocks, stride=9), :] = prods[:, LANES * c : LANES * (c + 1)]


def gather_kernel(back_ref, minus_ref, *pay_refs):
    count, _, share, bands = minus_ref.shape
    blocks = back_ref.shape[0] // 9
    groups = len(pay_refs)
    sums = [jnp.sum(back_ref[pl.ds(c, blocks, stride=9), :], axis=0, keepdims=True) for c in range(8)]
    edge_n, edge_m = jnp.concatenate(sums[:4], axis=0), jnp.concatenate(sums[4:], axis=0)
    tiles = back_ref[pl.ds(8, blocks, stride=9), :]
    lane = iota((blocks, bands), 1)
    spread = placed(tiles, jnp.where(lane // share == iota((blocks, bands), 0), 1.0, 0.0), ((0,), (0,)))
    spread = jnp.where(iota(spread.shape, 0) % share == iota(spread.shape, 1) % share, spread, 0.0)
    shape = (count * 2 * share, spread.shape[0])
    row, col = iota(shape, 0), iota(shape, 1)
    same = (row % share == col // (count * 2 * share)) & (row // share == (col // share) % (count * 2))
    sign = jnp.where((row // share) % 2 == 0, 1.0, -1.0)
    mirror = placed(jnp.where(same, sign, 0.0), spread, ((1,), (0,)))
    for k in range(count):
        for o in range(2):
            minus_ref[k, o] = mirror[(2 * k + o) * share : (2 * k + o + 1) * share]
    for d, ref in enumerate(pay_refs):
        piece = jnp.where(lax.rem(lax.axis_index(KZ) + d, groups) == groups - 1, edge_n, edge_m)
        if d == 1:
            ref[...] = jnp.zeros_like(ref)
            ref[pl.ds(0, 2 * share), :] = mirror[(count - 1) * 2 * share :]
            ref[pl.ds(2 * share, share), pl.ds(0, LANES)] = piece
        else:
            ref[...] = piece


def close_kernel(plus_ref, minus_ref, *refs):
    got_refs, plus_out, minus_out = refs[:-2], refs[-2], refs[-1]
    count, _, share, bands = plus_ref.shape
    groups = len(got_refs)
    here = lax.axis_index(KZ)
    got = [
        ref[pl.ds(2 * share, share), pl.ds(0, LANES)] if d == 1 else ref[...]
        for d, ref in enumerate(got_refs)
    ]
    plus_out[...] = plus_ref[...]
    for k in range(1, count):
        minus_out[k] = minus_ref[k - 1]
    for o in range(2):
        minus_out[0, o] = got_refs[1][pl.ds(o * share, share), :]

    @pl.when(here == groups - 1)
    def _():
        shape = (LANES, 2 * bands)
        row, col = iota(shape, 0), iota(shape, 1)
        half = LANES // 2
        rows = jnp.zeros((share, 2 * bands), F32)
        for j in range(groups):
            spot = (row // half == col // bands) & ((row % half) * groups + j == col % bands)
            rows = rows + placed(got[groups - 1 - j], jnp.where(spot, 1.0, 0.0), ((1,), (0,)))
        for o in range(2):
            plus_out[count - 1, o] = rows[:, o * bands : (o + 1) * bands]

    @pl.when(here == 0)
    def _():
        per = bands // LANES
        for j in range(groups):
            piece = got[(groups - j) % groups]
            for r in range(2 * per):
                minus_out[0, r // per, pl.ds(j, 1), pl.ds((r % per) * LANES, LANES)] = piece[r : r + 1]


def body(waves, pw_map):
    kz_dev, _, rows, _, bands = waves.shape
    n_kz, n_pw, n_x, n_z = (lax.axis_size(a) for a in (KZ, PW, "x", "z"))
    share = bands // n_pw
    planes = waves[:, 0].transpose(0, 2, 1, 3)

    def swap(x, axes):
        return lax.all_to_all(x, axes, 0, 0, tiled=True)

    def sent(x, pairs):
        return lax.ppermute(x, KZ, pairs)

    def around(x, d, ends=None):
        pairs = [(i, (i + d) % n_kz) for i in range(n_kz)]
        return sent(x, [p for p in pairs if ends is None or p[1] in ends])

    def beside(x):
        return lax.ppermute(x, "y_lo", [(0, 1), (1, 0)])

    def near(x):
        return lax.ppermute(x, "x", [(i, i ^ 1) for i in range(n_x)])

    def mirrored(x):
        return lax.ppermute(x, "x", [(i, n_x - 1 - i) for i in range(n_x)])

    plane = (planes.shape[1:], BF16)
    with jax.named_scope("deal"):
        digits = ((2 * rows // LANES, LANES), F32)
        *dealt, first, digits = call(
            deal_kernel, "deal", [((2 * n_pw, rows), BF16)] * (share - 1) + [plane, digits], (planes, pw_map),
            flops=4 * rows * bands * bands,
        )
        dealt = [dealt[0]] + [sent(dealt[j], [(0, j)]) for j in range(1, n_kz - 1)]

    with jax.named_scope("inner"):
        arriving = around(first, n_kz - 1)
        chunks = kz_dev * bands * share // LANES
        part = ((n_pw // 2, chunks, LANES), F32)
        *sums, final = call(
            terms_kernel, "terms", [part] * 4 + [plane], (planes, arriving), after=dealt[1:],
            flops=kz_dev * 8 * rows * bands * bands, scratch=[pltpu.VMEM((bands, 2 * bands), F32)],
        )
        terms = sums[0]
        sums = (sums[0], near(sums[1]), sums[2], beside(sums[3]))
        finals = [sent(final, [(n_kz - 1, j)]) for j in range(n_kz - 1)]

    with jax.named_scope("deal"):
        (load,) = call(
            load_kernel, "load", [((n_pw, 4 * rows // LANES, LANES), F32)], (digits, dealt[0], arriving, *dealt[1:]),
            after=(terms,),
        )
        spread = swap(load, PW)
    with jax.named_scope("pick"):
        (picked,) = call(
            pick_kernel, "pick", [((n_pw, 2 * rows // LANES, LANES), F32)], (spread,),
            flops=4 * n_pw * n_pw * rows * rows, scratch=[pltpu.VMEM((n_pw, rows), jnp.int32)] * 2,
        )

    with jax.named_scope("inner"):
        sums = call(fold_kernel, "fold", [((n_pw // 4, chunks, LANES), F32)] * 4, sums)
        sums = (sums[0], mirrored(sums[1]), sums[2], near(sums[3]))
        sums = call(fold_kernel, "fold", [((n_pw // 8, chunks, LANES), F32)] * 4, sums)
        sums = (sums[0], beside(sums[1]), sums[2], mirrored(sums[3]))
    with jax.named_scope("pick"):
        picked = swap(picked, ("x", "y_lo"))
    with jax.named_scope("inner"):
        (merged,) = call(
            merge_kernel, "merge", [((n_z, n_pw // n_z * 2 * rows // LANES + 2 * chunks, LANES), F32)],
            (picked, *sums), after=finals,
        )
        got = swap(merged, "z")

    with jax.named_scope("edge"):
        rows_out = ((kz_dev, 2, share, bands), F32)
        plus, out = call(
            edge_kernel, "edge", [rows_out, ((n_pw * 9, LANES), F32)], (got, final, *finals),
            flops=8 * n_pw * rows * bands,
            scratch=[
                pltpu.VMEM((n_pw, 2 * rows), F32),
                pltpu.VMEM((bands, 2 * n_pw), F32),
                pltpu.VMEM((kz_dev * 2 * share, bands), F32),
            ],
        )
        back = swap(out.reshape(n_pw, 1, 9 * LANES), PW).reshape(n_pw * 9, LANES)

    with jax.named_scope("close"):
        piece = ((share, LANES), F32)
        long = ((4 * share, bands), F32)
        minus, *pieces = call(gather_kernel, "gather", [rows_out, piece, long] + [piece] * (n_kz - 2), (back,))
        pieces = [pieces[0]] + [
            around(pieces[d], d, None if d == 1 else (0, n_kz - 1)) for d in range(1, n_kz)
        ]
        plus, minus = call(close_kernel, "close", [rows_out] * 2, (plus, minus, *pieces), far=(0, 1))
    return plus[:, None], minus[:, None]


def solution(mesh):
    fine = Mesh(mesh.devices.reshape(2, 2, 4, 2, 8), KZ + PW)
    out = P(KZ, None, None, PW, None)
    return jax.shard_map(
        body,
        mesh=fine,
        in_specs=(P(KZ, None, PW, None, None), P(None, PW)),
        out_specs=(out, out),
        check_vma=False,
    )
```

```python
import functools

import jax
import jax.numpy as jnp
from jax import lax
from jax.experimental import pallas as pl
from jax.experimental.pallas import tpu as pltpu
from jax.sharding import Mesh, PartitionSpec as P

KZ = ("y_hi", "core")
PW = ("x", "y_lo", "z")
F32, BF16 = jnp.float32, jnp.bfloat16
VMEM = pl.BlockSpec(memory_space=pltpu.VMEM)
AFTER = pl.BlockSpec(memory_space=pl.ANY)
LANES = 128


def iota(shape, axis):
    return lax.broadcasted_iota(jnp.int32, shape, axis)


def across(left, right, dims, precision=None):
    return lax.dot_general(left, right, (dims, ((), ())), precision=precision, preferred_element_type=F32)


def placed(left, right, dims):
    return across(left, right, dims, lax.Precision.HIGHEST)


def wide(real, imag):
    return jnp.concatenate(
        [jnp.concatenate([real, imag], axis=1), jnp.concatenate([imag, -real], axis=1)], axis=0
    )


def call(kernel, name, outs, operands, after=(), flops=0, scratch=(), far=()):
    outs = [jax.ShapeDtypeStruct(*o) if i in far else pltpu.VMEM(*o) for i, o in enumerate(outs)]
    size = sum(x.size * x.dtype.itemsize for x in operands)
    return pl.pallas_call(
        kernel,
        out_shape=outs,
        in_specs=[AFTER] * len(after) + [VMEM] * len(operands),
        out_specs=[VMEM] * len(outs),
        scratch_shapes=list(scratch),
        cost_estimate=pl.CostEstimate(flops=flops, bytes_accessed=2 * size, transcendentals=0),
        compiler_params=pltpu.CompilerParams(vmem_limit_bytes=16 << 20),
        name=name,
    )(*after, *(pltpu.with_memory_space_constraint(x, pltpu.VMEM) for x in operands))


def dealt_to(group, groups, bands):
    shape = (bands // groups, bands)
    return jnp.where(iota(shape, 1) == iota(shape, 0) * groups + group, 1.0, 0.0).astype(BF16)


def deal_kernel(planes_ref, *out_refs):
    plane_ref, first_ref, out_refs = planes_ref.at[0], out_refs[-1], out_refs[:-1]
    groups, bands = len(out_refs) + 1, plane_ref.shape[2]
    blocks = bands // groups
    for j, out_ref in enumerate(out_refs):
        for part in range(2):
            dealt = across(dealt_to(j, groups, bands), plane_ref[part], ((1,), (1,)))
            out_ref[pl.ds(part * blocks, blocks), :] = dealt.astype(BF16)
    first_ref[...] = plane_ref[...]


def terms_kernel(late, *refs):
    if late:
        planes_ref, arriving_ref, *out_refs, prod_ref = refs[-5:]
        count = planes_ref.shape[0]
        planes = [planes_ref.at[k] for k in range(count // 2, count)] + [arriving_ref]
    else:
        planes_ref, *out_refs, last_ref, prod_ref = refs[-5:]
        count = planes_ref.shape[0]
        planes = [planes_ref.at[k] for k in range(count // 2 + 1)]
        last_ref[...] = planes_ref[count - 1]
    _, rows, bands = planes[0].shape
    per, size = 2 * bands // LANES, out_refs[0].shape[0] // 4
    share = bands // (8 * size)
    here, side = lax.axis_index("x"), lax.axis_index("y_lo")
    near = here + 1 - 2 * lax.rem(here, 2)
    sides = (side, 1 - side)
    if late:
        order = [[(x, s) for x in (here, 3 - here, near, 3 - near)] for s in sides]
    else:
        order = [[(x, s) for x in xs for s in sides] for xs in ((here, 3 - here), (near, 3 - near))]
    for k in range(2):
        left, after = planes[k], planes[k + 1]
        prod_ref[...] = across(left[...].reshape(2 * rows, bands), wide(after[0], after[1]), ((0,), (0,)))
        for out_ref, places in zip(out_refs, order):
            for p, (x, s) in enumerate(places):
                first = pl.multiple_of((2 * x + s) * size * share, size * share)
                mine = prod_ref.at[pl.ds(first, size * share)]
                for i in range(size):
                    for c in range(per):
                        piece = mine[pl.ds(i * share, share), pl.ds(c * LANES, LANES)]
                        out_ref[p * size + i, pl.ds((k * per + c) * share, share), :] = piece


def load_kernel(*refs):
    digits_ref, own_ref, arriving_ref, *refs = refs[2:]
    out_ref = refs[-1]
    blocks = out_ref.shape[0]
    here, groups = lax.axis_index(KZ), len(refs) + 1
    mine = jnp.where(here == 0, own_ref[...].astype(F32), 0.0)
    for ref in refs[:-1]:
        mine = mine + ref[...].astype(F32)
    order = dealt_to(groups - 1, groups, arriving_ref.shape[2])
    last = [across(order, arriving_ref[part], ((1,), (1,))) for part in range(2)]
    mine = jnp.where(here == groups - 1, jnp.concatenate(last, axis=0), mine)
    per = mine.shape[1] // LANES
    for i, part in enumerate((mine[:blocks], mine[blocks:])):
        for c in range(per):
            out_ref[:, i * per + c, :] = part[:, c * LANES : (c + 1) * LANES]
    digits = digits_ref[...]
    for c in range(2 * per):
        out_ref[:, 2 * per + c, :] = jnp.broadcast_to(digits[c : c + 1], (blocks, LANES))


def pick_kernel(spread_ref, out_ref, hi_ref, lo_ref):
    blocks, width = hi_ref.shape
    per = width // LANES

    def part(i):
        return jnp.concatenate([spread_ref[:, i * per + c, :] for c in range(per)], axis=1)

    table = jnp.concatenate([part(0), part(1)], axis=0).astype(BF16)
    hi_ref[...] = part(2).astype(jnp.int32)
    lo_ref[...] = part(3)
    rows, owners = iota((width, width), 0).astype(F32).astype(BF16), iota((blocks, width), 0)
    one, zero = jnp.ones((), BF16), jnp.zeros((), BF16)

    def step(t, carry):
        base = pl.multiple_of(t * 8, 8)
        his, los = hi_ref[pl.ds(base, 8), :], lo_ref[pl.ds(base, 8), :].astype(BF16)
        real_rows, imag_rows = [], []
        for r in range(8):
            hot = jnp.where(rows == los[r : r + 1, :], one, zero)
            found = jnp.dot(table, hot, preferred_element_type=F32)
            mine = owners == his[r : r + 1, :]
            real_rows.append(jnp.sum(jnp.where(mine, found[:blocks], 0.0), axis=0, keepdims=True))
            imag_rows.append(jnp.sum(jnp.where(mine, found[blocks:], 0.0), axis=0, keepdims=True))
        for i, picked in enumerate((real_rows, imag_rows)):
            picked = jnp.concatenate(picked, axis=0)
            for c in range(per):
                out_ref[pl.ds(base, 8), i * per + c, :] = picked[:, c * LANES : (c + 1) * LANES]
        return carry

    lax.fori_loop(0, blocks // 8, step, 0)


def fold_kernel(*refs):
    in_refs, out_refs = refs[-8:-4], refs[-4:]
    half = out_refs[0].shape[0]
    for i in range(4):
        kept, got = in_refs[i // 2 * 2], in_refs[i // 2 * 2 + 1]
        part = pl.ds(i % 2 * half, half)
        out_refs[i][...] = kept[part] + got[part]


def pass_kernel(final_ref, *refs):
    fold_kernel(*refs[:-1])
    refs[-1][...] = final_ref[...]


def merge_kernel(final_ref, over_ref, picked_ref, *refs):
    sums_refs, out_ref, hand_ref = refs[:-2], refs[-2], refs[-1]
    hand_ref[...] = jnp.where(lax.axis_index(KZ) == 0, over_ref[...], final_ref[...])
    far, rows = out_ref.shape[0], sums_refs[0].shape[1]
    near, chunks = picked_ref.shape[0] // far, picked_ref.shape[1]
    for p in range(near):
        for z in range(far):
            out_ref[z, pl.ds(p * chunks, chunks), :] = picked_ref[p * far + z]
    for i in range(2):
        out_ref[:, pl.ds(near * chunks + i * rows, rows), :] = sums_refs[2 * i][...] + sums_refs[2 * i + 1][...]


def edge_kernel(got_ref, own_ref, other_ref, *refs):
    (plus_ref, out_ref, moved_ref, turn_ref, rows_ref) = refs
    count, _, share, bands = plus_ref.shape
    blocks, width = moved_ref.shape
    far = got_ref.shape[0]
    chunks, near, per = width // LANES, blocks // far, bands // LANES
    here = lax.axis_index(KZ)

    total = got_ref[0, pl.ds(near * chunks, count * 2 * per * share), :]
    for z in range(1, far):
        total = total + got_ref[z, pl.ds(near * chunks, count * 2 * per * share), :]
    for k in range(count):
        for o in range(2):
            for c in range(per):
                first = ((k * 2 + o) * per + c) * share
                piece = total[first : first + share]
                plus_ref[k, o, :, pl.ds(c * LANES, LANES)] = piece
                rows_ref[pl.ds((k * 2 + o) * share, share), pl.ds(c * LANES, LANES)] = piece
    place, band = iota((bands, bands), 0), iota((bands, bands), 1)
    order = jnp.where(band == (place % blocks) * share + place // blocks, 1.0, 0.0)
    tiles = placed(order, rows_ref[...], ((1,), (1,)))
    tiles = jnp.concatenate([tiles[i * blocks : (i + 1) * blocks] for i in range(share)], axis=1)
    out_ref[pl.ds(8, blocks, stride=9), :] = tiles

    final = jnp.where((here == 0) | (here == lax.axis_size(KZ) - 1), own_ref[...], other_ref[...])
    for p in range(near):
        for c in range(chunks):
            moved_ref[pl.ds(p * far, far), pl.ds(c * LANES, LANES)] = got_ref[:, p * chunks + c, :]
    moved = moved_ref[...].astype(BF16)
    prods = jnp.dot(moved, wide(final[0], final[1]), preferred_element_type=F32)
    turn_ref[...] = jnp.concatenate([prods[:, :bands].T, -prods[:, bands:].T], axis=1)
    for c in range(4):
        out_ref[pl.ds(c, blocks, stride=9), :] = turn_ref[pl.ds(c, blocks, stride=4), :]
        out_ref[pl.ds(4 + c, blocks, stride=9), :] = prods[:, LANES * c : LANES * (c + 1)]


def gather_kernel(back_ref, minus_ref, *pay_refs):
    count, _, share, bands = minus_ref.shape
    blocks = back_ref.shape[0] // 9
    groups = len(pay_refs)
    sums = [jnp.sum(back_ref[pl.ds(c, blocks, stride=9), :], axis=0, keepdims=True) for c in range(8)]
    edge_n, edge_m = jnp.concatenate(sums[:4], axis=0), jnp.concatenate(sums[4:], axis=0)
    tiles = back_ref[pl.ds(8, blocks, stride=9), :]
    lane = iota((blocks, bands), 1)
    spread = placed(tiles, jnp.where(lane // share == iota((blocks, bands), 0), 1.0, 0.0), ((0,), (0,)))
    spread = jnp.where(iota(spread.shape, 0) % share == iota(spread.shape, 1) % share, spread, 0.0)
    shape = (count * 2 * share, spread.shape[0])
    row, col = iota(shape, 0), iota(shape, 1)
    same = (row % share == col // (count * 2 * share)) & (row // share == (col // share) % (count * 2))
    sign = jnp.where((row // share) % 2 == 0, 1.0, -1.0)
    mirror = placed(jnp.where(same, sign, 0.0), spread, ((1,), (0,)))
    for k in range(count):
        for o in range(2):
            minus_ref[k, o] = mirror[(2 * k + o) * share : (2 * k + o + 1) * share]
    for d, ref in enumerate(pay_refs):
        piece = jnp.where(lax.rem(lax.axis_index(KZ) + d, groups) == groups - 1, edge_n, edge_m)
        ref[...] = jnp.zeros_like(ref)
        if d == 1:
            ref[pl.ds(0, 2 * share), :] = mirror[(count - 1) * 2 * share :]
        ref[pl.ds(2 * share, share), pl.ds(0, LANES)] = piece


def close_kernel(plus_ref, minus_ref, *refs):
    got_refs, plus_out, minus_out = refs[:-2], refs[-2], refs[-1]
    count, _, share, bands = plus_ref.shape
    groups = len(got_refs)
    here = lax.axis_index(KZ)
    got = [ref[pl.ds(2 * share, share), pl.ds(0, LANES)] for ref in got_refs]
    plus_out[...] = plus_ref[...]
    for k in range(1, count):
        minus_out[k] = minus_ref[k - 1]
    for o in range(2):
        minus_out[0, o] = got_refs[1][pl.ds(o * share, share), :]

    @pl.when(here == groups - 1)
    def _():
        shape = (LANES, 2 * bands)
        row, col = iota(shape, 0), iota(shape, 1)
        half = LANES // 2
        rows = jnp.zeros((share, 2 * bands), F32)
        for j in range(groups):
            spot = (row // half == col // bands) & ((row % half) * groups + j == col % bands)
            rows = rows + placed(got[groups - 1 - j], jnp.where(spot, 1.0, 0.0), ((1,), (0,)))
        for o in range(2):
            plus_out[count - 1, o] = rows[:, o * bands : (o + 1) * bands]

    @pl.when(here == 0)
    def _():
        per = bands // LANES
        for j in range(groups):
            piece = got[(groups - j) % groups]
            for r in range(2 * per):
                minus_out[0, r // per, pl.ds(j, 1), pl.ds((r % per) * LANES, LANES)] = piece[r : r + 1]


def body(waves, pw_map):
    kz_dev, _, rows, _, bands = waves.shape
    n_kz, n_pw, n_x, n_z = (lax.axis_size(a) for a in (KZ, PW, "x", "z"))
    share = bands // n_pw
    planes = waves[:, 0].transpose(0, 2, 1, 3)

    def swap(x, axes):
        return lax.all_to_all(x, axes, 0, 0, tiled=True)

    def sent(x, pairs):
        return lax.ppermute(x, KZ, pairs)

    def around(x, d, ends=None):
        pairs = [(i, (i + d) % n_kz) for i in range(n_kz)]
        return sent(x, [p for p in pairs if ends is None or p[1] in ends])

    def beside(x):
        return lax.ppermute(x, "y_lo", [(0, 1), (1, 0)])

    def near(x):
        return lax.ppermute(x, "x", [(i, i ^ 1) for i in range(n_x)])

    def mirrored(x):
        return lax.ppermute(x, "x", [(i, n_x - 1 - i) for i in range(n_x)])

    plane = (planes.shape[1:], BF16)
    with jax.named_scope("deal"):
        *dealt, first = call(
            deal_kernel, "deal", [((2 * n_pw, rows), BF16)] * (share - 1) + [plane], (planes,),
            flops=4 * rows * bands * bands,
        )
        dealt = [dealt[0]] + [sent(dealt[j], [(0, j)]) for j in range(n_kz - 2, 0, -1)]
        digits = jnp.stack([pw_map[0] // rows, pw_map[0] % rows]).astype(F32).reshape(-1, LANES)

    with jax.named_scope("inner"):
        arriving = around(first, n_kz - 1)
        chunks = kz_dev * bands * share // LANES

        def make_terms(late, operands, after, more):
            return call(
                functools.partial(terms_kernel, late), "terms", [((n_pw // 2, chunks, LANES), F32)] * 2 + more,
                operands, after=after, flops=16 * rows * bands * bands, scratch=[pltpu.VMEM((bands, 2 * bands), F32)],
            )

        *early, final = make_terms(False, (planes,), (), [plane])
        late = make_terms(True, (planes, arriving), dealt[1:], [])
        sums = (early[0], near(early[1]), late[0], beside(late[1]))

    with jax.named_scope("deal"):
        (load,) = call(
            load_kernel, "load", [((n_pw, 4 * rows // LANES, LANES), F32)], (digits, dealt[0], arriving, *dealt[1:]),
            after=(early[0], late[0]),
        )
        spread = swap(load, PW)
    with jax.named_scope("pick"):
        (picked,) = call(
            pick_kernel, "pick", [((n_pw, 2 * rows // LANES, LANES), F32)], (spread,),
            flops=4 * n_pw * n_pw * rows * rows,
            scratch=[pltpu.VMEM((n_pw, rows), jnp.int32), pltpu.VMEM((n_pw, rows), F32)],
        )

    with jax.named_scope("inner"):
        *sums, final = call(
            pass_kernel, "fold", [((n_pw // 4, chunks, LANES), F32)] * 4 + [plane], (final, *sums)
        )
        over = sent(final, [(n_kz - 1, 0)])
        sums = (sums[0], mirrored(sums[1]), sums[2], near(sums[3]))
        sums = call(fold_kernel, "fold", [((n_pw // 8, chunks, LANES), F32)] * 4, sums, after=(picked,))
        sums = (sums[0], beside(sums[1]), sums[2], mirrored(sums[3]))
    with jax.named_scope("pick"):
        picked = swap(picked, ("x", "y_lo"))
    with jax.named_scope("inner"):
        merged, hand = call(
            merge_kernel, "merge", [((n_z, n_pw // n_z * 2 * rows // LANES + 2 * chunks, LANES), F32), plane],
            (final, over, picked, *sums),
        )
        across_chip = sent(hand, [(0, 1), (n_kz - 1, n_kz - 2)])
        got = swap(merged, "z")

    with jax.named_scope("edge"):
        rows_out = ((kz_dev, 2, share, bands), F32)
        plus, out = call(
            edge_kernel, "edge", [rows_out, ((n_pw * 9, LANES), F32)], (got, hand, across_chip),
            flops=8 * n_pw * rows * bands,
            scratch=[
                pltpu.VMEM((n_pw, 2 * rows), F32),
                pltpu.VMEM((bands, 2 * n_pw), F32),
                pltpu.VMEM((kz_dev * 2 * share, bands), F32),
            ],
        )
        back = swap(out.reshape(n_pw, 1, 9 * LANES), PW).reshape(n_pw * 9, LANES)

    with jax.named_scope("close"):
        pieces = [((4 * share, bands), F32)] * 2 + [((6 * share, bands), F32)] * (n_kz - 2)
        minus, *pieces = call(gather_kernel, "gather", [rows_out] + pieces, (back,))
        for d in (2, 3, 1):
            pieces[d] = around(pieces[d], d, None if d == 1 else (0, n_kz - 1))
        plus, minus = call(close_kernel, "close", [rows_out] * 2, (plus, minus, *pieces), far=(0, 1))
    return plus[:, None], minus[:, None]


def solution(mesh):
    fine = Mesh(mesh.devices.reshape(2, 2, 4, 2, 8), KZ + PW)
    out = P(KZ, None, None, PW, None)
    return jax.shard_map(
        body,
        mesh=fine,
        in_specs=(P(KZ, None, PW, None, None), P(None, PW)),
        out_specs=(out, out),
        check_vma=False,
    )
```

```python
import functools

import jax
import jax.numpy as jnp
from jax import lax
from jax.experimental import pallas as pl
from jax.experimental.pallas import tpu as pltpu
from jax.sharding import Mesh, PartitionSpec as P

KZ = ("y_hi", "core")
PW = ("x", "y_lo", "z")
F32, BF16 = jnp.float32, jnp.bfloat16
VMEM = pl.BlockSpec(memory_space=pltpu.VMEM)
AFTER = pl.BlockSpec(memory_space=pl.ANY)
LANES = 128


def iota(shape, axis):
    return lax.broadcasted_iota(jnp.int32, shape, axis)


def across(left, right, dims, precision=None):
    return lax.dot_general(left, right, (dims, ((), ())), precision=precision, preferred_element_type=F32)


def placed(left, right, dims):
    return across(left, right, dims, lax.Precision.HIGHEST)


def wide(real, imag):
    return jnp.concatenate(
        [jnp.concatenate([real, imag], axis=1), jnp.concatenate([imag, -real], axis=1)], axis=0
    )


def call(kernel, name, outs, operands, after=(), flops=0, scratch=(), far=()):
    outs = [jax.ShapeDtypeStruct(*o) if i in far else pltpu.VMEM(*o) for i, o in enumerate(outs)]
    size = sum(x.size * x.dtype.itemsize for x in operands)
    return pl.pallas_call(
        kernel,
        out_shape=outs,
        in_specs=[AFTER] * len(after) + [VMEM] * len(operands),
        out_specs=[VMEM] * len(outs),
        scratch_shapes=list(scratch),
        cost_estimate=pl.CostEstimate(flops=flops, bytes_accessed=2 * size, transcendentals=0),
        compiler_params=pltpu.CompilerParams(vmem_limit_bytes=16 << 20),
        name=name,
    )(*after, *(pltpu.with_memory_space_constraint(x, pltpu.VMEM) for x in operands))


def dealt_to(group, groups, bands):
    shape = (bands // groups, bands)
    return jnp.where(iota(shape, 1) == iota(shape, 0) * groups + group, 1.0, 0.0).astype(BF16)


def deal_kernel(planes_ref, *out_refs):
    plane_ref, first_ref, out_refs = planes_ref.at[0], out_refs[-1], out_refs[:-1]
    groups, bands = len(out_refs) + 1, plane_ref.shape[2]
    blocks = bands // groups
    for j, out_ref in enumerate(out_refs):
        for part in range(2):
            dealt = across(dealt_to(j, groups, bands), plane_ref[part], ((1,), (1,)))
            out_ref[pl.ds(part * blocks, blocks), :] = dealt.astype(BF16)
    first_ref[...] = plane_ref[...]


def terms_kernel(late, *refs):
    if late:
        planes_ref, arriving_ref, *out_refs, prod_ref = refs[-5:]
        count = planes_ref.shape[0]
        planes = [planes_ref.at[k] for k in range(count // 2, count)] + [arriving_ref]
    else:
        planes_ref, *out_refs, last_ref, prod_ref = refs[-5:]
        count = planes_ref.shape[0]
        planes = [planes_ref.at[k] for k in range(count // 2 + 1)]
        last_ref[...] = planes_ref[count - 1]
    _, rows, bands = planes[0].shape
    per, size = 2 * bands // LANES, out_refs[0].shape[0] // 4
    share = bands // (8 * size)
    here, side = lax.axis_index("x"), lax.axis_index("y_lo")
    near = here + 1 - 2 * lax.rem(here, 2)
    sides = (side, 1 - side)
    if late:
        order = [[(x, s) for x in (here, 3 - here, near, 3 - near)] for s in sides]
    else:
        order = [[(x, s) for x in xs for s in sides] for xs in ((here, 3 - here), (near, 3 - near))]
    for k in range(2):
        left, after = planes[k], planes[k + 1]
        prod_ref[...] = across(left[...].reshape(2 * rows, bands), wide(after[0], after[1]), ((0,), (0,)))
        for out_ref, places in zip(out_refs, order):
            for p, (x, s) in enumerate(places):
                first = pl.multiple_of((2 * x + s) * size * share, size * share)
                mine = prod_ref.at[pl.ds(first, size * share)]
                for i in range(size):
                    for c in range(per):
                        piece = mine[pl.ds(i * share, share), pl.ds(c * LANES, LANES)]
                        out_ref[p * size + i, pl.ds((k * per + c) * share, share), :] = piece


def load_kernel(*refs):
    index_ref, own_ref, arriving_ref, *refs = refs[2:]
    out_ref = refs[-1]
    blocks = own_ref.shape[0] // 2
    here, groups = lax.axis_index(KZ), len(refs) + 1
    mine = jnp.where(here == 0, own_ref[...].astype(F32), 0.0)
    for ref in refs[:-1]:
        mine = mine + ref[...].astype(F32)
    order = dealt_to(groups - 1, groups, arriving_ref.shape[2])
    last = [across(order, arriving_ref[part], ((1,), (1,))) for part in range(2)]
    mine = jnp.where(here == groups - 1, jnp.concatenate(last, axis=0), mine)
    per = mine.shape[1] // LANES
    for i, part in enumerate((mine[:blocks], mine[blocks:])):
        for c in range(per):
            out_ref[pl.ds(i * per + c, blocks, stride=3 * per), :] = part[:, c * LANES : (c + 1) * LANES]
    index = index_ref[...]
    for c in range(per):
        row = jnp.broadcast_to(index[:, c * LANES : (c + 1) * LANES], (blocks, LANES))
        out_ref[pl.ds(2 * per + c, blocks, stride=3 * per), :] = row


def pick_kernel(spread_ref, out_ref, hi_ref, lo_ref):
    blocks, width = hi_ref.shape
    per = width // LANES

    def part(i):
        rows = [spread_ref[pl.ds(i * per + c, blocks, stride=3 * per), :] for c in range(per)]
        return jnp.concatenate(rows, axis=1)

    table = jnp.concatenate([part(0), part(1)], axis=0).astype(BF16)
    index = part(2).astype(jnp.int32)
    hi_ref[...] = index // width
    lo_ref[...] = (index % width).astype(F32)
    rows, owners = iota((width, width), 0).astype(F32).astype(BF16), iota((blocks, width), 0)
    one, zero = jnp.ones((), BF16), jnp.zeros((), BF16)

    def step(t, carry):
        base = pl.multiple_of(t * 16, 16)
        his, los = hi_ref[pl.ds(base, 16), :], lo_ref[pl.ds(base, 16), :].astype(BF16)
        real_rows, imag_rows = [], []
        for r in range(16):
            hot = jnp.where(rows == los[r : r + 1, :], one, zero)
            found = jnp.dot(table, hot, preferred_element_type=F32)
            mine = owners == his[r : r + 1, :]
            real_rows.append(jnp.sum(jnp.where(mine, found[:blocks], 0.0), axis=0, keepdims=True))
            imag_rows.append(jnp.sum(jnp.where(mine, found[blocks:], 0.0), axis=0, keepdims=True))
        for i, picked in enumerate((real_rows, imag_rows)):
            picked = jnp.concatenate(picked, axis=0)
            for c in range(per):
                out_ref[pl.ds(base, 16), i * per + c, :] = picked[:, c * LANES : (c + 1) * LANES]
        return carry

    lax.fori_loop(0, blocks // 16, step, 0)


def fold_kernel(*refs):
    in_refs, out_refs = refs[-8:-4], refs[-4:]
    half = out_refs[0].shape[0]
    for i in range(4):
        kept, got = in_refs[i // 2 * 2], in_refs[i // 2 * 2 + 1]
        part = pl.ds(i % 2 * half, half)
        out_refs[i][...] = kept[part] + got[part]


def pass_kernel(final_ref, *refs):
    fold_kernel(*refs[:-1])
    refs[-1][...] = final_ref[...]


def merge_kernel(final_ref, over_ref, picked_ref, *refs):
    sums_refs, out_ref, hand_ref = refs[:-2], refs[-2], refs[-1]
    hand_ref[...] = jnp.where(lax.axis_index(KZ) == 0, over_ref[...], final_ref[...])
    far, rows = out_ref.shape[0], sums_refs[0].shape[1]
    near, chunks = picked_ref.shape[0] // far, picked_ref.shape[1]
    for p in range(near):
        for z in range(far):
            out_ref[z, pl.ds(p * chunks, chunks), :] = picked_ref[p * far + z]
    for i in range(2):
        out_ref[:, pl.ds(near * chunks + i * rows, rows), :] = sums_refs[2 * i][...] + sums_refs[2 * i + 1][...]


def edge_kernel(got_ref, own_ref, other_ref, *refs):
    (plus_ref, out_ref, moved_ref, turn_ref, rows_ref) = refs
    count, _, share, bands = plus_ref.shape
    blocks, width = moved_ref.shape
    far = got_ref.shape[0]
    chunks, near, per = width // LANES, blocks // far, bands // LANES
    here = lax.axis_index(KZ)

    total = got_ref[0, pl.ds(near * chunks, count * 2 * per * share), :]
    for z in range(1, far):
        total = total + got_ref[z, pl.ds(near * chunks, count * 2 * per * share), :]
    for k in range(count):
        for o in range(2):
            for c in range(per):
                first = ((k * 2 + o) * per + c) * share
                piece = total[first : first + share]
                plus_ref[k, o, :, pl.ds(c * LANES, LANES)] = piece
                rows_ref[pl.ds((k * 2 + o) * share, share), pl.ds(c * LANES, LANES)] = piece
    place, band = iota((bands, bands), 0), iota((bands, bands), 1)
    order = jnp.where(band == (place % blocks) * share + place // blocks, 1.0, 0.0)
    tiles = placed(order, rows_ref[...], ((1,), (1,)))
    tiles = jnp.concatenate([tiles[i * blocks : (i + 1) * blocks] for i in range(share)], axis=1)
    out_ref[pl.ds(8, blocks, stride=9), :] = tiles

    final = jnp.where((here == 0) | (here == lax.axis_size(KZ) - 1), own_ref[...], other_ref[...])
    for p in range(near):
        for c in range(chunks):
            moved_ref[pl.ds(p * far, far), pl.ds(c * LANES, LANES)] = got_ref[:, p * chunks + c, :]
    moved = moved_ref[...].astype(BF16)
    prods = jnp.dot(moved, wide(final[0], final[1]), preferred_element_type=F32)
    turn_ref[...] = jnp.concatenate([prods[:, :bands].T, -prods[:, bands:].T], axis=1)
    for c in range(4):
        out_ref[pl.ds(c, blocks, stride=9), :] = turn_ref[pl.ds(c, blocks, stride=4), :]
        out_ref[pl.ds(4 + c, blocks, stride=9), :] = prods[:, LANES * c : LANES * (c + 1)]


def gather_kernel(back_ref, minus_ref, *pay_refs):
    count, _, share, bands = minus_ref.shape
    blocks = back_ref.shape[0] // 9
    groups = len(pay_refs)
    sums = [jnp.sum(back_ref[pl.ds(c, blocks, stride=9), :], axis=0, keepdims=True) for c in range(8)]
    edge_n, edge_m = jnp.concatenate(sums[:4], axis=0), jnp.concatenate(sums[4:], axis=0)
    tiles = back_ref[pl.ds(8, blocks, stride=9), :]
    lane = iota((blocks, bands), 1)
    spread = placed(tiles, jnp.where(lane // share == iota((blocks, bands), 0), 1.0, 0.0), ((0,), (0,)))
    spread = jnp.where(iota(spread.shape, 0) % share == iota(spread.shape, 1) % share, spread, 0.0)
    shape = (count * 2 * share, spread.shape[0])
    row, col = iota(shape, 0), iota(shape, 1)
    same = (row % share == col // (count * 2 * share)) & (row // share == (col // share) % (count * 2))
    sign = jnp.where((row // share) % 2 == 0, 1.0, -1.0)
    mirror = placed(jnp.where(same, sign, 0.0), spread, ((1,), (0,)))
    for k in range(count):
        for o in range(2):
            minus_ref[k, o] = mirror[(2 * k + o) * share : (2 * k + o + 1) * share]
    for d, ref in enumerate(pay_refs):
        piece = jnp.where(lax.rem(lax.axis_index(KZ) + d, groups) == groups - 1, edge_n, edge_m)
        ref[...] = jnp.zeros_like(ref)
        if d == 1:
            ref[pl.ds(0, 2 * share), :] = mirror[(count - 1) * 2 * share :]
        ref[pl.ds(2 * share, share), pl.ds(0, LANES)] = piece


def close_kernel(plus_ref, minus_ref, *refs):
    got_refs, plus_out, minus_out = refs[:-2], refs[-2], refs[-1]
    count, _, share, bands = plus_ref.shape
    groups = len(got_refs)
    here = lax.axis_index(KZ)
    got = [ref[pl.ds(2 * share, share), pl.ds(0, LANES)] for ref in got_refs]
    plus_out[...] = plus_ref[...]
    for k in range(1, count):
        minus_out[k] = minus_ref[k - 1]
    for o in range(2):
        minus_out[0, o] = got_refs[1][pl.ds(o * share, share), :]

    @pl.when(here == groups - 1)
    def _():
        shape = (LANES, 2 * bands)
        row, col = iota(shape, 0), iota(shape, 1)
        half = LANES // 2
        rows = jnp.zeros((share, 2 * bands), F32)
        for j in range(groups):
            spot = (row // half == col // bands) & ((row % half) * groups + j == col % bands)
            rows = rows + placed(got[groups - 1 - j], jnp.where(spot, 1.0, 0.0), ((1,), (0,)))
        for o in range(2):
            plus_out[count - 1, o] = rows[:, o * bands : (o + 1) * bands]

    @pl.when(here == 0)
    def _():
        per = bands // LANES
        for j in range(groups):
            piece = got[(groups - j) % groups]
            for r in range(2 * per):
                minus_out[0, r // per, pl.ds(j, 1), pl.ds((r % per) * LANES, LANES)] = piece[r : r + 1]


def body(waves, pw_map):
    kz_dev, _, rows, _, bands = waves.shape
    n_kz, n_pw, n_x, n_z = (lax.axis_size(a) for a in (KZ, PW, "x", "z"))
    share = bands // n_pw
    planes = waves[:, 0].transpose(0, 2, 1, 3)

    def swap(x, axes):
        return lax.all_to_all(x, axes, 0, 0, tiled=True)

    def sent(x, pairs):
        return lax.ppermute(x, KZ, pairs)

    def around(x, d, ends=None):
        pairs = [(i, (i + d) % n_kz) for i in range(n_kz)]
        return sent(x, [p for p in pairs if ends is None or p[1] in ends])

    def beside(x):
        return lax.ppermute(x, "y_lo", [(0, 1), (1, 0)])

    def near(x):
        return lax.ppermute(x, "x", [(i, i ^ 1) for i in range(n_x)])

    def mirrored(x):
        return lax.ppermute(x, "x", [(i, n_x - 1 - i) for i in range(n_x)])

    plane = (planes.shape[1:], BF16)
    with jax.named_scope("deal"):
        *dealt, first = call(
            deal_kernel, "deal", [((2 * n_pw, rows), BF16)] * (share - 1) + [plane], (planes,),
            flops=4 * rows * bands * bands,
        )
        dealt = [dealt[0]] + [sent(dealt[j], [(0, j)]) for j in range(n_kz - 2, 0, -1)]

    with jax.named_scope("inner"):
        arriving = around(first, n_kz - 1)
        chunks = kz_dev * bands * share // LANES

        def make_terms(late, operands, after, more):
            return call(
                functools.partial(terms_kernel, late), "terms", [((n_pw // 2, chunks, LANES), F32)] * 2 + more,
                operands, after=after, flops=16 * rows * bands * bands, scratch=[pltpu.VMEM((bands, 2 * bands), F32)],
            )

        *early, final = make_terms(False, (planes,), (), [plane])
        late = make_terms(True, (planes, arriving), dealt[1:], [])
        sums = (early[0], near(early[1]), late[0], beside(late[1]))

    with jax.named_scope("deal"):
        (load,) = call(
            load_kernel, "load", [((n_pw * 3 * rows // LANES, LANES), F32)],
            (pw_map.astype(F32), dealt[0], arriving, *dealt[1:]),
            after=(early[0], late[0]),
        )
        spread = swap(load.reshape(n_pw, 1, -1), PW).reshape(load.shape)
    with jax.named_scope("pick"):
        (picked,) = call(
            pick_kernel, "pick", [((n_pw, 2 * rows // LANES, LANES), F32)], (spread,),
            flops=4 * n_pw * n_pw * rows * rows,
            scratch=[pltpu.VMEM((n_pw, rows), jnp.int32), pltpu.VMEM((n_pw, rows), F32)],
        )

    with jax.named_scope("inner"):
        *sums, final = call(
            pass_kernel, "fold", [((n_pw // 4, chunks, LANES), F32)] * 4 + [plane], (final, *sums)
        )
        over = sent(final, [(n_kz - 1, 0)])
        sums = (sums[0], mirrored(sums[1]), sums[2], near(sums[3]))
        sums = call(fold_kernel, "fold", [((n_pw // 8, chunks, LANES), F32)] * 4, sums, after=(picked,))
        sums = (sums[0], beside(sums[1]), sums[2], mirrored(sums[3]))
    with jax.named_scope("pick"):
        picked = swap(picked, ("x", "y_lo"))
    with jax.named_scope("inner"):
        merged, hand = call(
            merge_kernel, "merge", [((n_z, n_pw // n_z * 2 * rows // LANES + 2 * chunks, LANES), F32), plane],
            (final, over, picked, *sums),
        )
        across_chip = sent(hand, [(0, 1), (n_kz - 1, n_kz - 2)])
        got = swap(merged, "z")

    with jax.named_scope("edge"):
        rows_out = ((kz_dev, 2, share, bands), F32)
        plus, out = call(
            edge_kernel, "edge", [rows_out, ((n_pw * 9, LANES), F32)], (got, hand, across_chip),
            flops=8 * n_pw * rows * bands,
            scratch=[
                pltpu.VMEM((n_pw, 2 * rows), F32),
                pltpu.VMEM((bands, 2 * n_pw), F32),
                pltpu.VMEM((kz_dev * 2 * share, bands), F32),
            ],
        )
        back = swap(out.reshape(n_pw, 1, 9 * LANES), PW).reshape(n_pw * 9, LANES)

    with jax.named_scope("close"):
        pieces = [((4 * share, bands), F32)] * 2 + [((6 * share, bands), F32)] * (n_kz - 2)
        minus, *pieces = call(gather_kernel, "gather", [rows_out] + pieces, (back,))
        for d in (2, 3, 1):
            pieces[d] = around(pieces[d], d, None if d == 1 else (0, n_kz - 1))
        plus, minus = call(close_kernel, "close", [rows_out] * 2, (plus, minus, *pieces), far=(0, 1))
    return plus[:, None], minus[:, None]


def solution(mesh):
    fine = Mesh(mesh.devices.reshape(2, 2, 4, 2, 8), KZ + PW)
    out = P(KZ, None, None, PW, None)
    return jax.shard_map(
        body,
        mesh=fine,
        in_specs=(P(KZ, None, PW, None, None), P(None, PW)),
        out_specs=(out, out),
        check_vma=False,
    )
```

```python
import functools

import jax
import jax.numpy as jnp
from jax import lax
from jax.experimental import pallas as pl
from jax.experimental.pallas import tpu as pltpu
from jax.sharding import Mesh, PartitionSpec as P

KZ = ("y_hi", "core")
PW = ("x", "y_lo", "z")
F32, BF16 = jnp.float32, jnp.bfloat16
VMEM = pl.BlockSpec(memory_space=pltpu.VMEM)
AFTER = pl.BlockSpec(memory_space=pl.ANY)
LANES = 128


def iota(shape, axis):
    return lax.broadcasted_iota(jnp.int32, shape, axis)


def across(left, right, dims, precision=None):
    return lax.dot_general(left, right, (dims, ((), ())), precision=precision, preferred_element_type=F32)


def placed(left, right, dims):
    return across(left, right, dims, lax.Precision.HIGHEST)


def wide(real, imag):
    return jnp.concatenate(
        [jnp.concatenate([real, imag], axis=1), jnp.concatenate([imag, -real], axis=1)], axis=0
    )


def call(kernel, name, outs, operands, after=(), flops=0, scratch=(), far=()):
    outs = [jax.ShapeDtypeStruct(*o) if i in far else pltpu.VMEM(*o) for i, o in enumerate(outs)]
    size = sum(x.size * x.dtype.itemsize for x in operands)
    return pl.pallas_call(
        kernel,
        out_shape=outs,
        in_specs=[AFTER] * len(after) + [VMEM] * len(operands),
        out_specs=[VMEM] * len(outs),
        scratch_shapes=list(scratch),
        cost_estimate=pl.CostEstimate(flops=flops, bytes_accessed=2 * size, transcendentals=0),
        compiler_params=pltpu.CompilerParams(vmem_limit_bytes=16 << 20),
        name=name,
    )(*after, *(pltpu.with_memory_space_constraint(x, pltpu.VMEM) for x in operands))


def dealt_to(group, groups, bands):
    shape = (bands // groups, bands)
    return jnp.where(iota(shape, 1) == iota(shape, 0) * groups + group, 1.0, 0.0).astype(BF16)


def deal_kernel(planes_ref, *out_refs):
    plane_ref, first_ref, out_refs = planes_ref.at[0], out_refs[-1], out_refs[:-1]
    groups, bands = len(out_refs) + 1, plane_ref.shape[2]
    blocks = bands // groups
    for j, out_ref in enumerate(out_refs):
        for part in range(2):
            dealt = across(dealt_to(j, groups, bands), plane_ref[part], ((1,), (1,)))
            out_ref[pl.ds(part * blocks, blocks), :] = dealt.astype(BF16)
    first_ref[...] = plane_ref[...]


def terms_kernel(late, *refs):
    if late:
        planes_ref, arriving_ref, *out_refs, prod_ref = refs[-5:]
        count = planes_ref.shape[0]
        planes = [planes_ref.at[k] for k in range(count // 2, count)] + [arriving_ref]
    else:
        planes_ref, *out_refs, last_ref, prod_ref = refs[-5:]
        count = planes_ref.shape[0]
        planes = [planes_ref.at[k] for k in range(count // 2 + 1)]
        last_ref[...] = planes_ref[count - 1]
    _, rows, bands = planes[0].shape
    per, size = 2 * bands // LANES, out_refs[0].shape[0] // 4
    share = bands // (8 * size)
    here, side = lax.axis_index("x"), lax.axis_index("y_lo")
    near = here + 1 - 2 * lax.rem(here, 2)
    sides = (side, 1 - side)
    if late:
        order = [[(x, s) for x in (here, 3 - here, near, 3 - near)] for s in sides]
    else:
        order = [[(x, s) for x in xs for s in sides] for xs in ((here, 3 - here), (near, 3 - near))]
    for k in range(2):
        left, after = planes[k], planes[k + 1]
        prod_ref[...] = across(left[...].reshape(2 * rows, bands), wide(after[0], after[1]), ((0,), (0,)))
        for out_ref, places in zip(out_refs, order):
            for p, (x, s) in enumerate(places):
                first = pl.multiple_of((2 * x + s) * size * share, size * share)
                mine = prod_ref.at[pl.ds(first, size * share)]
                for i in range(size):
                    for c in range(per):
                        piece = mine[pl.ds(i * share, share), pl.ds(c * LANES, LANES)]
                        out_ref[p * size + i, pl.ds((k * per + c) * share, share), :] = piece


def load_kernel(*refs):
    index_ref, own_ref, arriving_ref, *refs = refs[2:]
    out_ref = refs[-1]
    blocks = own_ref.shape[0] // 2
    here, groups = lax.axis_index(KZ), len(refs) + 1
    mine = jnp.where(here == 0, own_ref[...].astype(F32), 0.0)
    for ref in refs[:-1]:
        mine = mine + ref[...].astype(F32)
    order = dealt_to(groups - 1, groups, arriving_ref.shape[2])
    last = [across(order, arriving_ref[part], ((1,), (1,))) for part in range(2)]
    mine = jnp.where(here == groups - 1, jnp.concatenate(last, axis=0), mine)
    per = mine.shape[1] // LANES
    for i, part in enumerate((mine[:blocks], mine[blocks:])):
        for c in range(per):
            out_ref[pl.ds(i * per + c, blocks, stride=3 * per), :] = part[:, c * LANES : (c + 1) * LANES]
    index = index_ref[...]
    for c in range(per):
        row = jnp.broadcast_to(index[:, c * LANES : (c + 1) * LANES], (blocks, LANES))
        out_ref[pl.ds(2 * per + c, blocks, stride=3 * per), :] = row


def pick_kernel(spread_ref, out_ref, hi_ref, lo_ref):
    blocks, width = hi_ref.shape
    per = width // LANES

    def part(i):
        rows = [spread_ref[pl.ds(i * per + c, blocks, stride=3 * per), :] for c in range(per)]
        return jnp.concatenate(rows, axis=1)

    table = jnp.concatenate([part(0), part(1)], axis=0).astype(BF16)
    index = part(2).astype(jnp.int32)
    hi_ref[...] = index // width
    lo_ref[...] = (index % width).astype(F32)
    rows, owners = iota((width, width), 0).astype(F32).astype(BF16), iota((blocks, width), 0)
    one, zero = jnp.ones((), BF16), jnp.zeros((), BF16)

    def step(t, carry):
        base = pl.multiple_of(t * 16, 16)
        his, los = hi_ref[pl.ds(base, 16), :], lo_ref[pl.ds(base, 16), :].astype(BF16)
        real_rows, imag_rows = [], []
        for r in range(16):
            hot = jnp.where(rows == los[r : r + 1, :], one, zero)
            found = jnp.dot(table, hot, preferred_element_type=F32)
            mine = owners == his[r : r + 1, :]
            real_rows.append(jnp.sum(jnp.where(mine, found[:blocks], 0.0), axis=0, keepdims=True))
            imag_rows.append(jnp.sum(jnp.where(mine, found[blocks:], 0.0), axis=0, keepdims=True))
        for i, picked in enumerate((real_rows, imag_rows)):
            picked = jnp.concatenate(picked, axis=0)
            for c in range(per):
                out_ref[pl.ds(base, 16), i * per + c, :] = picked[:, c * LANES : (c + 1) * LANES]
        return carry

    lax.fori_loop(0, blocks // 16, step, 0)


def fold_kernel(*refs):
    in_refs, out_refs = refs[-8:-4], refs[-4:]
    half = out_refs[0].shape[0]
    for i in range(4):
        kept, got = in_refs[i // 2 * 2], in_refs[i // 2 * 2 + 1]
        part = pl.ds(i % 2 * half, half)
        out_refs[i][...] = kept[part] + got[part]


def pass_kernel(final_ref, *refs):
    fold_kernel(*refs[:-1])
    refs[-1][...] = final_ref[...]


def merge_kernel(final_ref, over_ref, picked_ref, *refs):
    sums_refs, out_ref, hand_ref = refs[:-2], refs[-2], refs[-1]
    hand_ref[...] = jnp.where(lax.axis_index(KZ) == 0, over_ref[...], final_ref[...])
    far, rows = out_ref.shape[0], sums_refs[0].shape[1]
    near, chunks = picked_ref.shape[0] // far, picked_ref.shape[1]
    for p in range(near):
        for z in range(far):
            out_ref[z, pl.ds(p * chunks, chunks), :] = picked_ref[p * far + z]
    for i in range(2):
        out_ref[:, pl.ds(near * chunks + i * rows, rows), :] = sums_refs[2 * i][...] + sums_refs[2 * i + 1][...]


def edge_kernel(got_ref, own_ref, other_ref, *refs):
    (plus_ref, out_ref, moved_ref, turn_ref, rows_ref) = refs
    count, _, share, bands = plus_ref.shape
    blocks, width = moved_ref.shape
    far = got_ref.shape[0]
    chunks, near, per = width // LANES, blocks // far, bands // LANES
    here = lax.axis_index(KZ)

    total = got_ref[0, pl.ds(near * chunks, count * 2 * per * share), :]
    for z in range(1, far):
        total = total + got_ref[z, pl.ds(near * chunks, count * 2 * per * share), :]
    for k in range(count):
        for o in range(2):
            for c in range(per):
                first = ((k * 2 + o) * per + c) * share
                piece = total[first : first + share]
                plus_ref[k, o, :, pl.ds(c * LANES, LANES)] = piece
                rows_ref[pl.ds((k * 2 + o) * share, share), pl.ds(c * LANES, LANES)] = piece
    place, band = iota((bands, bands), 0), iota((bands, bands), 1)
    order = jnp.where(band == (place % blocks) * share + place // blocks, 1.0, 0.0)
    tiles = placed(order, rows_ref[...], ((1,), (1,)))
    tiles = jnp.concatenate([tiles[i * blocks : (i + 1) * blocks] for i in range(share)], axis=1)
    out_ref[pl.ds(8, blocks, stride=9), :] = tiles

    final = jnp.where((here == 0) | (here == lax.axis_size(KZ) - 1), own_ref[...], other_ref[...])
    for p in range(near):
        for c in range(chunks):
            moved_ref[pl.ds(p * far, far), pl.ds(c * LANES, LANES)] = got_ref[:, p * chunks + c, :]
    moved = moved_ref[...].astype(BF16)
    prods = jnp.dot(moved, wide(final[0], final[1]), preferred_element_type=F32)
    turn_ref[...] = jnp.concatenate([prods[:, :bands].T, -prods[:, bands:].T], axis=1)
    for c in range(4):
        out_ref[pl.ds(c, blocks, stride=9), :] = turn_ref[pl.ds(c, blocks, stride=4), :]
        out_ref[pl.ds(4 + c, blocks, stride=9), :] = prods[:, LANES * c : LANES * (c + 1)]


def gather_kernel(back_ref, minus_ref, *pay_refs):
    count, _, share, bands = minus_ref.shape
    blocks = back_ref.shape[0] // 9
    groups = len(pay_refs)
    sums = [jnp.sum(back_ref[pl.ds(c, blocks, stride=9), :], axis=0, keepdims=True) for c in range(8)]
    edge_n, edge_m = jnp.concatenate(sums[:4], axis=0), jnp.concatenate(sums[4:], axis=0)
    tiles = back_ref[pl.ds(8, blocks, stride=9), :]
    lane = iota((blocks, bands), 1)
    spread = placed(tiles, jnp.where(lane // share == iota((blocks, bands), 0), 1.0, 0.0), ((0,), (0,)))
    spread = jnp.where(iota(spread.shape, 0) % share == iota(spread.shape, 1) % share, spread, 0.0)
    shape = (count * 2 * share, spread.shape[0])
    row, col = iota(shape, 0), iota(shape, 1)
    same = (row % share == col // (count * 2 * share)) & (row // share == (col // share) % (count * 2))
    sign = jnp.where((row // share) % 2 == 0, 1.0, -1.0)
    mirror = placed(jnp.where(same, sign, 0.0), spread, ((1,), (0,)))
    for k in range(count):
        for o in range(2):
            minus_ref[k, o] = mirror[(2 * k + o) * share : (2 * k + o + 1) * share]
    for d, ref in enumerate(pay_refs):
        piece = jnp.where(lax.rem(lax.axis_index(KZ) + d, groups) == groups - 1, edge_n, edge_m)
        ref[...] = jnp.zeros_like(ref)
        if d == 1:
            ref[pl.ds(0, 2 * share), :] = mirror[(count - 1) * 2 * share :]
        ref[pl.ds(2 * share, share), pl.ds(0, LANES)] = piece


def close_kernel(plus_ref, minus_ref, *refs):
    got_refs, plus_out, minus_out = refs[:-2], refs[-2], refs[-1]
    count, _, share, bands = plus_ref.shape
    groups = len(got_refs)
    here = lax.axis_index(KZ)
    got = [ref[pl.ds(2 * share, share), pl.ds(0, LANES)] for ref in got_refs]
    plus_out[...] = plus_ref[...]
    for k in range(1, count):
        minus_out[k] = minus_ref[k - 1]
    for o in range(2):
        minus_out[0, o] = got_refs[1][pl.ds(o * share, share), :]

    @pl.when(here == groups - 1)
    def _():
        shape = (LANES, 2 * bands)
        row, col = iota(shape, 0), iota(shape, 1)
        half = LANES // 2
        rows = jnp.zeros((share, 2 * bands), F32)
        for j in range(groups):
            spot = (row // half == col // bands) & ((row % half) * groups + j == col % bands)
            rows = rows + placed(got[groups - 1 - j], jnp.where(spot, 1.0, 0.0), ((1,), (0,)))
        for o in range(2):
            plus_out[count - 1, o] = rows[:, o * bands : (o + 1) * bands]

    @pl.when(here == 0)
    def _():
        per = bands // LANES
        for j in range(groups):
            piece = got[(groups - j) % groups]
            for r in range(2 * per):
                minus_out[0, r // per, pl.ds(j, 1), pl.ds((r % per) * LANES, LANES)] = piece[r : r + 1]


def body(waves, pw_map):
    kz_dev, _, rows, _, bands = waves.shape
    n_kz, n_pw, n_x, n_z = (lax.axis_size(a) for a in (KZ, PW, "x", "z"))
    share = bands // n_pw
    planes = waves[:, 0].transpose(0, 2, 1, 3)

    def swap(x, axes):
        return lax.all_to_all(x, axes, 0, 0, tiled=True)

    def sent(x, pairs):
        return lax.ppermute(x, KZ, pairs)

    def around(x, d, ends=None):
        pairs = [(i, (i + d) % n_kz) for i in range(n_kz)]
        return sent(x, [p for p in pairs if ends is None or p[1] in ends])

    def beside(x):
        return lax.ppermute(x, "y_lo", [(0, 1), (1, 0)])

    def near(x):
        return lax.ppermute(x, "x", [(i, i ^ 1) for i in range(n_x)])

    def mirrored(x):
        return lax.ppermute(x, "x", [(i, n_x - 1 - i) for i in range(n_x)])

    plane = (planes.shape[1:], BF16)
    with jax.named_scope("deal"):
        *dealt, first = call(
            deal_kernel, "deal", [((2 * n_pw, rows), BF16)] * (share - 1) + [plane], (planes,),
            flops=4 * rows * bands * bands,
        )
        dealt = [dealt[0]] + [sent(dealt[j], [(0, j)]) for j in range(n_kz - 2, 0, -1)]

    with jax.named_scope("inner"):
        arriving = around(first, n_kz - 1)
        chunks = kz_dev * bands * share // LANES

        def make_terms(late, operands, after, more):
            return call(
                functools.partial(terms_kernel, late), "terms", [((n_pw // 2, chunks, LANES), F32)] * 2 + more,
                operands, after=after, flops=16 * rows * bands * bands, scratch=[pltpu.VMEM((bands, 2 * bands), F32)],
            )

        *early, final = make_terms(False, (planes,), (), [plane])
        late = make_terms(True, (planes, arriving), dealt[1:], [])
        sums = (early[0], near(early[1]), late[0], beside(late[1]))

    with jax.named_scope("deal"):
        (load,) = call(
            load_kernel, "load", [((n_pw * 3 * rows // LANES, LANES), F32)],
            (pw_map.astype(F32), dealt[0], arriving, *dealt[1:]),
            after=(early[0], late[0]),
        )
        spread = swap(load.reshape(n_pw, 1, -1), PW).reshape(load.shape)
    with jax.named_scope("pick"):
        (picked,) = call(
            pick_kernel, "pick", [((n_pw, 2 * rows // LANES, LANES), F32)], (spread,),
            flops=4 * n_pw * n_pw * rows * rows,
            scratch=[pltpu.VMEM((n_pw, rows), jnp.int32), pltpu.VMEM((n_pw, rows), F32)],
        )

    with jax.named_scope("inner"):
        *sums, final = call(
            pass_kernel, "fold", [((n_pw // 4, chunks, LANES), F32)] * 4 + [plane], (final, *sums)
        )
        over = sent(final, [(n_kz - 1, 0)])
        sums = (sums[0], mirrored(sums[1]), sums[2], near(sums[3]))
        sums = call(fold_kernel, "fold", [((n_pw // 8, chunks, LANES), F32)] * 4, sums, after=(picked,))
        sums = (sums[0], beside(sums[1]), sums[2], mirrored(sums[3]))
    with jax.named_scope("pick"):
        picked = swap(picked, ("x", "y_lo"))
    with jax.named_scope("inner"):
        merged, hand = call(
            merge_kernel, "merge", [((n_z, n_pw // n_z * 2 * rows // LANES + 2 * chunks, LANES), F32), plane],
            (final, over, picked, *sums),
        )
        across_chip = sent(hand, [(0, 1), (n_kz - 1, n_kz - 2)])
        got = swap(merged, "z")

    with jax.named_scope("edge"):
        rows_out = ((kz_dev, 2, share, bands), F32)
        plus, out = call(
            edge_kernel, "edge", [rows_out, ((n_pw * 9, LANES), F32)], (got, hand, across_chip),
            flops=8 * n_pw * rows * bands,
            scratch=[
                pltpu.VMEM((n_pw, 2 * rows), F32),
                pltpu.VMEM((bands, 2 * n_pw), F32),
                pltpu.VMEM((kz_dev * 2 * share, bands), F32),
            ],
        )
        back = swap(out.reshape(n_pw, 1, 9 * LANES), PW).reshape(n_pw * 9, LANES)

    with jax.named_scope("close"):
        pieces = [((3 * share, bands), F32)] * 2 + [((4 * share, bands), F32)] * (n_kz - 2)
        minus, *pieces = call(gather_kernel, "gather", [rows_out] + pieces, (back,))
        for d in (2, 3, 1):
            pieces[d] = around(pieces[d], d, None if d == 1 else (0, n_kz - 1))
        plus, minus = call(close_kernel, "close", [rows_out] * 2, (plus, minus, *pieces), far=(0, 1))
    return plus[:, None], minus[:, None]


def solution(mesh):
    fine = Mesh(mesh.devices.reshape(2, 2, 4, 2, 8), KZ + PW)
    out = P(KZ, None, None, PW, None)
    return jax.shard_map(
        body,
        mesh=fine,
        in_specs=(P(KZ, None, PW, None, None), P(None, PW)),
        out_specs=(out, out),
        check_vma=False,
    )
```
